32 devices in a mesh: group: 2 (over x), expert: 16 (over z, y, core).
Axes of the slice: x: 2, y: 2, z: 4, core: 2. Of those that a mesh axis runs over, the one named last changes fastest.
Arguments:
- queries: bfloat16 [512, 4096], P(('group', 'expert')), parts along dimension 0, may hold values from -30 to 30
- fresh_key_rows: bfloat16 [512, 256], P(('group', 'expert')), parts along dimension 0, may hold values from -6 to 6
- fresh_value_rows: bfloat16 [512, 256], P(('group', 'expert')), parts along dimension 0, may hold values from -6 to 6
- key_cache_pages: bfloat16 [1024, 64, 256], P(('group', 'expert')), parts along dimension 0, may hold values from -6 to 6
- value_cache_pages: bfloat16 [1024, 64, 256], P(('group', 'expert')), parts along dimension 0, may hold values from -6 to 6
- sequence_page_table: int32 [32, 16], P(('group', 'expert')), parts along dimension 0, may hold values from 1 to 12, 32 in all within a row
- last_page_fill: int32 [512], P(('group', 'expert')), parts along dimension 0, may hold values from 1 to 64
- local_page_ranking: int32 [32, 32], P(('group', 'expert')), parts along dimension 0, may hold values from 0 to 31, each once within a row
- residual: bfloat16 [512, 4096], P(('group', 'expert')), parts along dimension 0, may hold values from -3 to 3
- out_weight: bfloat16 [4096, 4096], P(None, 'expert'), may hold values from -0.09375 to 0.09375
- norm_gain: bfloat16 [4096], replicated, may hold values from 0.25 to 1.75
- routes: int32 [512, 2], P(('group', 'expert')), parts along dimension 0, may hold values from 0 to 3, all different within a row; in each aligned block of 16 rows (0 to 15, 16 to 31, ...) at most 12 rows name the same one
- route_weight: float32 [512, 2], P(('group', 'expert')), parts along dimension 0, may hold values from 0.1 to 0.5
- w_gate: bfloat16 [16, 4096, 384], P('expert'), may hold values from -0.09375 to 0.09375
- w_up: bfloat16 [16, 4096, 384], P('expert'), may hold values from -0.09375 to 0.09375
- w_down: bfloat16 [16, 384, 4096], P('expert'), may hold values from -0.15625 to 0.15625
Outputs:
- layer_out: bfloat16 [512, 4096], P(('group', 'expert')), parts along dimension 0
The draws below stay inside these ranges and needn't reach their ends.
There are 2 independent parts, one for each index of `group`. The reference program is written for one: setup_inputs(seed, part) draws one part's arguments, and reference() takes and returns one part's arrays. A program takes and returns all parts, laid end to end along the dimension named above; an argument that names none is the same for every part. Nothing has to cross between parts.
Inputs may be any that keep to these rules, and one draw needn't show every extreme that they name: `routes`: each row names 2 different experts. Among the 16 rows of one device no expert is named more than 12 times, and in every draw some device names some expert exactly 12 times. `sequence_page_table`: each row gives the page counts of one device's 16 sequences; they sum to 32, and the largest is exactly 12. `local_page_ranking`: each row lists the 32 local pages of one device once each.
All inputs are finite; a program needn't handle non-finite values.
Results may differ from the reference program's by a relative error of at most 0.008.
Values may be sent and summed in bfloat16 or wider, within the bound.
A program may use at most 128 MiB of HBM per device.

```python
import math
import jax
import jax.numpy as jnp
import numpy as np
from jax import lax

D = 4096
QUERY_HEADS = 32
KEY_VALUE_HEADS = 2
HEAD_SIZE = 128
FF = 1536
SHARDS = 4
PAGE_TOKENS = 64
LOCAL_ROW_COUNT = 16
FF_DEV = 384
EXPERTS = 4
TOP = 2
CAP = 12
LOCAL_PAGE_POOL = 32
MAXP = 12
SEQUENCE_COUNT = 256
N_EXPERT = 16


def draw_queries(key, part):
    key = jax.random.fold_in(key, 1)
    base_offset = jnp.clip(jax.random.normal(key, (SEQUENCE_COUNT, QUERY_HEADS * HEAD_SIZE), jnp.float32), -6.0, 6.0)
    return base_offset.astype(jnp.bfloat16)


def draw_fresh_key_rows(key, part):
    key = jax.random.fold_in(key, 2)
    base_offset = jnp.clip(jax.random.normal(key, (SEQUENCE_COUNT, KEY_VALUE_HEADS * HEAD_SIZE), jnp.float32), -6.0, 6.0)
    return base_offset.astype(jnp.bfloat16)


def draw_key_cache_pages(key, part):
    key = jax.random.fold_in(key, 3)
    entry_count = N_EXPERT * LOCAL_PAGE_POOL
    base_offset = jnp.clip(jax.random.normal(key, (entry_count, PAGE_TOKENS, KEY_VALUE_HEADS * HEAD_SIZE), jnp.float32), -6.0, 6.0)
    return base_offset.astype(jnp.bfloat16)


def set_ends(result, stream_key, low, high):
    index_at = [jax.random.randint(jax.random.fold_in(stream_key, axis), (), 0, length) for axis, length in enumerate(result.shape)]
    longest = result.shape.index(max(result.shape))
    beside = index_at[:longest] + [(index_at[longest] + 1) % result.shape[longest]] + index_at[longest + 1:]
    return result.at[tuple(index_at)].set(low).at[tuple(beside)].set(high)


def levels(own_key, dims, pieces, smallest, largest):
    def one(dim, parts):
        steps = jax.random.uniform(jax.random.fold_in(jax.random.fold_in(own_key, 6), dim), (parts,), jnp.float32, smallest / len(pieces), largest / len(pieces))
        return jnp.repeat(jnp.exp(steps), dims[dim] // parts).reshape((-1,) + (1,) * (len(dims) - dim - 1))

    factor_of = one(*pieces[0])
    for cut in pieces[1:]:
        factor_of = factor_of * one(*cut)
    return factor_of


def split_up(amount, total, reach, slope):
    weights = [(1 << 20) // math.isqrt(rank ** slope) + 1 for rank in range(2, amount + 1)]
    spare, counts = total - reach - (amount - 1), [1] * (amount - 1)
    while spare > 0:
        candidates = [i for i in range(amount - 1) if counts[i] < reach]
        whole, budget = sum([weights[i] for i in candidates]), spare
        for i in candidates:
            extra = min(reach - counts[i], max(1, budget * weights[i] // whole), spare)
            counts[i] = counts[i] + extra
            spare = spare - extra
    return np.array([reach] + counts)


def ragged(own_key, count, total, bound, lean):
    if count == 2:
        one = jax.random.randint(own_key, (), max(1, total - bound), min(bound, total - 1) + 1)
        return jnp.stack([one, total - one])
    sizes = jnp.asarray(split_up(count, total, bound, lean), jnp.int32)
    pairs = (count - 1) // 2
    source_of, receiver = sizes[1:1 + 2 * pairs:2], sizes[2:2 + 2 * pairs:2]
    margin = jnp.minimum(source_of - 1, bound - receiver)
    passed = jax.random.randint(jax.random.fold_in(own_key, 1), (pairs,), 0, 1 << 20) % (margin + 1)
    sizes = sizes.at[1:1 + 2 * pairs:2].set(source_of - passed).at[2:2 + 2 * pairs:2].set(receiver + passed)
    return sizes[jax.random.permutation(jax.random.fold_in(own_key, 2), count)]


def assign_block(own_key, own, number, rows, number_of, top, most, skew):
    ranking = jax.random.permutation(own_key, number_of)
    crowded, usual = portions_of(number_of, rows * top, most, skew, True), portions_of(number_of, rows * top, most, skew, False)
    places = jnp.arange(number_of)

    def named(tallies, turn):
        used = int((tallies > 0).sum())
        fixed = max(1, used // 4)
        shifted = fixed + (places - fixed + turn * (used - fixed)) % max(1, number_of - fixed)
        return jnp.zeros((number_of,), jnp.int32).at[ranking[jnp.where(places < fixed, places, shifted)]].set(jnp.asarray(tallies, jnp.int32))

    tallies = jnp.where(number % 4 == 0, named(crowded, number // 4), named(usual, number - number // 4 - 1))
    mixed = jax.random.permutation(jax.random.fold_in(own, 3), number_of)
    donor, taker = mixed[0:number_of // 2 * 2:2], mixed[1:number_of // 2 * 2:2]
    room = jnp.minimum(tallies[donor] - 1, most - tallies[taker]) // 2
    room = jnp.where((donor == ranking[0]) | (taker == ranking[0]) | (tallies[taker] == 0), 0, jnp.maximum(room, 0))
    shifted = jax.random.randint(jax.random.fold_in(own, 4), (number_of // 2,), 0, 1 << 20) % (room + 1)
    tallies = tallies.at[donor].add(-shifted).at[taker].add(shifted)
    members = jnp.searchsorted(jnp.cumsum(tallies), jnp.arange(rows * top), side="right").astype(jnp.int32)
    grid = members.reshape(top, rows).T
    grid = grid[jax.random.permutation(jax.random.fold_in(own, 1), rows)]
    turn = jax.random.randint(jax.random.fold_in(own, 2), (rows, 1), 0, top)
    return jnp.take_along_axis(grid, (jnp.arange(top)[None, :] + turn) % top, axis=1)


def portions_of(count, total, bound, lean, full):
    loads = [(1 << 20) // math.isqrt(grade ** lean) + 1 for grade in range(1, count + 1)]
    largest = bound if full else min(bound, max(-(-total // count), total * loads[0] // sum(loads)))
    least = 1 if total - largest >= count - 1 else 0
    counts, surplus = [largest] + [least] * (count - 1), total - largest - least * (count - 1)
    while surplus > 0:
        movable = [i for i in range(1, count) if counts[i] < largest] or [i for i in range(1, count) if counts[i] < bound]
        mass, remaining = sum([loads[i] for i in movable]), surplus
        for i in movable:
            extra = min(bound - counts[i], max(1, remaining * loads[i] // mass), surplus)
            counts[i] = counts[i] + extra
            surplus = surplus - extra
    return np.array(counts)


def noise(key, shape, width, bound, cuts=(), kind=jnp.bfloat16):
    result = jax.random.normal(key, shape, jnp.float32) * width
    if len(cuts) > 0:
        result = levels(key, shape, cuts, -0.22, 0.18) * result
    return jnp.clip(result, min=-bound, max=bound).astype(kind)


def setup_inputs(seed: int = 0, part: int = 0) -> dict:
    arg_keys = jax.random.split(jax.random.key(seed), 17)
    part_keys = jax.random.split(jax.random.fold_in(arg_keys[16], part), 17)
    queries = draw_queries(jax.random.fold_in(jax.random.fold_in(arg_keys[16], part), 71), part)
    fresh_key_rows = draw_fresh_key_rows(jax.random.fold_in(jax.random.fold_in(arg_keys[16], part), 71), part)
    fresh_value_rows = noise(part_keys[2], (SEQUENCE_COUNT, KEY_VALUE_HEADS * HEAD_SIZE), 1.0, 6.0, ((0, 16),))
    key_cache_pages = draw_key_cache_pages(jax.random.fold_in(jax.random.fold_in(arg_keys[16], part), 71), part)
    value_cache_pages = noise(part_keys[4], (N_EXPERT * LOCAL_PAGE_POOL, PAGE_TOKENS, KEY_VALUE_HEADS * HEAD_SIZE), 1.0, 6.0, ((0, 16),))
    sequence_page_table = jax.vmap(lambda own: ragged(own, LOCAL_ROW_COUNT, LOCAL_PAGE_POOL, MAXP, 2))(jax.random.split(part_keys[5], N_EXPERT)).reshape((N_EXPERT, LOCAL_ROW_COUNT)).astype(jnp.int32)
    last_page_fill = set_ends(jax.random.randint(part_keys[6], (SEQUENCE_COUNT,), 1, PAGE_TOKENS + 1), jax.random.fold_in(part_keys[6], 1), 1, PAGE_TOKENS).astype(jnp.int32)
    local_page_ranking = jax.vmap(lambda own: jax.random.permutation(own, LOCAL_PAGE_POOL))(jax.random.split(part_keys[7], N_EXPERT)).reshape((N_EXPERT, LOCAL_PAGE_POOL)).astype(jnp.int32)
    residual = noise(part_keys[8], (SEQUENCE_COUNT, D), 0.5, 3.0, ((0, 16),))
    out_weight = noise(arg_keys[9], (QUERY_HEADS * HEAD_SIZE, D), (QUERY_HEADS * HEAD_SIZE) ** -0.5, 0.09375, ((1, 16),))
    norm_gain = jnp.clip(1.0 + 0.15 * jax.random.normal(arg_keys[10], (D,), jnp.float32), 0.25, 1.75).astype(jnp.bfloat16)
    routes_keys = jax.random.split(jax.random.fold_in(part_keys[11], 1), SEQUENCE_COUNT // LOCAL_ROW_COUNT)
    routes_turns = jax.random.permutation(jax.random.fold_in(part_keys[11], 3), SEQUENCE_COUNT // LOCAL_ROW_COUNT)
    routes = jax.vmap(lambda own, number: assign_block(jax.random.fold_in(part_keys[11], 2), own, number, LOCAL_ROW_COUNT, EXPERTS, TOP, CAP, 1))(routes_keys, routes_turns).reshape((SEQUENCE_COUNT, TOP))
    route_weight = jnp.clip(0.1 + 0.4 * jax.random.uniform(part_keys[12], (SEQUENCE_COUNT, TOP), jnp.float32) ** levels(part_keys[12], (SEQUENCE_COUNT, TOP), ((0, 16),), -0.2, 0.2), 0.1, 0.5)
    w_gate = noise(arg_keys[13], (N_EXPERT, D, FF_DEV), D ** -0.5, 0.09375, ((0, 16),))
    w_up = noise(arg_keys[14], (N_EXPERT, D, FF_DEV), D ** -0.5, 0.09375, ((0, 16),))
    w_down = noise(arg_keys[15], (N_EXPERT, FF_DEV, D), FF ** -0.5, 0.15625, ((0, 16),))
    return {"queries": queries, "fresh_key_rows": fresh_key_rows, "fresh_value_rows": fresh_value_rows, "key_cache_pages": key_cache_pages, "value_cache_pages": value_cache_pages, "sequence_page_table": sequence_page_table, "last_page_fill": last_page_fill, "local_page_ranking": local_page_ranking, "residual": residual, "out_weight": out_weight, "norm_gain": norm_gain, "routes": routes, "route_weight": route_weight, "w_gate": w_gate, "w_up": w_up, "w_down": w_down}


def local_attention(queries, fresh_key_rows, fresh_value_rows, key_cache_pages, value_cache_pages, sequence_page_table, last_page_fill, local_page_ranking):
    count_of_rows = queries.shape[0]
    pooled_pages = local_page_ranking.shape[0]
    page_length = key_cache_pages.shape[1]
    query_group_width = QUERY_HEADS // KEY_VALUE_HEADS
    sequence_page_table = sequence_page_table.astype(jnp.int32)
    first_page = (jnp.cumsum(sequence_page_table) - sequence_page_table).astype(jnp.int32)
    page_slot = jnp.arange(pooled_pages, dtype=jnp.int32)
    row_ids = jnp.arange(count_of_rows, dtype=jnp.int32)
    inside = (page_slot[:, None] >= first_page[None, :]) & (page_slot[:, None] < (first_page + sequence_page_table)[None, :])
    owner_slot = lax.optimization_barrier(jnp.sum(jnp.where(inside, row_ids[None, :], 0), axis=1)).astype(jnp.int32)
    index_slot = (page_slot - lax.optimization_barrier(jnp.sum(jnp.where(inside, first_page[None, :], 0), axis=1))).astype(jnp.int32)
    placed = local_page_ranking[None, :] == page_slot[:, None]
    page_owner = lax.optimization_barrier(jnp.sum(jnp.where(placed, owner_slot[None, :], 0), axis=1)).astype(jnp.int32)
    page_index = lax.optimization_barrier(jnp.sum(jnp.where(placed, index_slot[None, :], 0), axis=1)).astype(jnp.int32)
    cached = (sequence_page_table - 1) * page_length + last_page_fill.astype(jnp.int32)
    token_place = page_index[:, None] * page_length + jnp.arange(page_length, dtype=jnp.int32)[None, :]
    visible = (page_owner[None, :, None] == row_ids[:, None, None]) & (token_place[None, :, :] < cached[:, None, None])
    visible = visible.reshape(count_of_rows, pooled_pages * page_length)
    score_scale = 1.0 / math.sqrt(HEAD_SIZE)
    query_head_rows = queries.astype(jnp.float32).reshape(count_of_rows, KEY_VALUE_HEADS, query_group_width, HEAD_SIZE)
    key_matrix = key_cache_pages.astype(jnp.float32).reshape(pooled_pages * page_length, KEY_VALUE_HEADS, HEAD_SIZE)
    value_matrix = value_cache_pages.astype(jnp.float32).reshape(pooled_pages * page_length, KEY_VALUE_HEADS, HEAD_SIZE)
    scores = jnp.einsum('rhgd,thd->rhgt', query_head_rows, key_matrix) * score_scale
    self_score = jnp.einsum('jqnu,jqu->jqn', query_head_rows, fresh_key_rows.astype(jnp.float32).reshape(count_of_rows, KEY_VALUE_HEADS, HEAD_SIZE)) * score_scale
    scores = jnp.where(visible[:, None, None, :], scores, -jnp.inf)
    highest = jnp.maximum(lax.optimization_barrier(jnp.max(scores, axis=-1)), self_score)
    raised = jnp.exp(scores - highest[..., None])
    own_raised = jnp.exp(self_score - highest)
    denominator = lax.optimization_barrier(jnp.sum(raised, axis=-1)) + own_raised
    weights = (raised / denominator[..., None]).astype(jnp.bfloat16)
    self_weight = (own_raised / denominator).astype(jnp.bfloat16)
    mixed_output = jnp.einsum('rhgt,thd->rhgd', weights.astype(jnp.float32), value_matrix)
    mixed_output = mixed_output + self_weight.astype(jnp.float32)[..., None] * fresh_value_rows.astype(jnp.float32).reshape(count_of_rows, KEY_VALUE_HEADS, 1, HEAD_SIZE)
    return mixed_output.reshape(count_of_rows, QUERY_HEADS * HEAD_SIZE).astype(jnp.bfloat16)

def reference(queries, fresh_key_rows, fresh_value_rows, key_cache_pages, value_cache_pages, sequence_page_table, last_page_fill, local_page_ranking, residual, out_weight, norm_gain, routes, route_weight, w_gate, w_up, w_down):
    device_list = N_EXPERT
    block_list = (queries.reshape(device_list, LOCAL_ROW_COUNT, QUERY_HEADS * HEAD_SIZE), fresh_key_rows.reshape(device_list, LOCAL_ROW_COUNT, KEY_VALUE_HEADS * HEAD_SIZE), fresh_value_rows.reshape(device_list, LOCAL_ROW_COUNT, KEY_VALUE_HEADS * HEAD_SIZE), key_cache_pages.reshape(device_list, LOCAL_PAGE_POOL, PAGE_TOKENS, KEY_VALUE_HEADS * HEAD_SIZE), value_cache_pages.reshape(device_list, LOCAL_PAGE_POOL, PAGE_TOKENS, KEY_VALUE_HEADS * HEAD_SIZE), sequence_page_table, last_page_fill.reshape(device_list, LOCAL_ROW_COUNT), local_page_ranking)
    head_out = lax.map(lambda block: local_attention(*block), block_list).reshape(SEQUENCE_COUNT, QUERY_HEADS * HEAD_SIZE)
    projected = jnp.dot(head_out, out_weight, preferred_element_type=jnp.float32).astype(jnp.bfloat16)
    hidden = residual.astype(jnp.float32) + projected.astype(jnp.float32)
    normed = (hidden * lax.rsqrt(lax.optimization_barrier(jnp.mean(hidden * hidden, axis=-1, keepdims=True)) + 1e-06) * norm_gain.astype(jnp.float32)).astype(jnp.bfloat16)
    expert_ids = jnp.arange(EXPERTS, dtype=jnp.int32)
    weight_table = lax.optimization_barrier(jnp.sum(jnp.where(routes[:, :, None] == expert_ids[None, None, :], route_weight[:, :, None], 0.0), axis=1))

    def add_shard(total, shard):
        gate_now = lax.dynamic_index_in_dim(w_gate, shard, 0, keepdims=False)
        up_now = lax.dynamic_index_in_dim(w_up, shard, 0, keepdims=False)
        down_now = lax.dynamic_index_in_dim(w_down, shard, 0, keepdims=False)
        gate = jnp.dot(normed, gate_now, preferred_element_type=jnp.float32)
        upward = jnp.dot(normed, up_now, preferred_element_type=jnp.float32)
        act = (jax.nn.silu(gate) * upward).astype(jnp.bfloat16)
        part = jnp.dot(act, down_now, preferred_element_type=jnp.float32).astype(jnp.bfloat16)
        column = lax.dynamic_index_in_dim(weight_table, shard // SHARDS, 1, keepdims=False)
        return (total + column[:, None] * part.astype(jnp.float32), None)
    total, unused = lax.scan(add_shard, jnp.zeros((SEQUENCE_COUNT, D), jnp.float32), jnp.arange(N_EXPERT, dtype=jnp.int32))
    return (hidden + total).astype(jnp.bfloat16)
```

```python
import functools
import math

import jax
import jax.numpy as jnp
from jax import lax
from jax.experimental import pallas as pl
from jax.experimental.pallas import tpu as pltpu
from jax.sharding import PartitionSpec as P

D = 4096
QUERY_HEADS = 32
KEY_VALUE_HEADS = 2
HEAD_SIZE = 128
SHARDS = 4
CAP = 12


def local_attention(
    queries,
    fresh_key_rows,
    fresh_value_rows,
    key_cache_pages,
    value_cache_pages,
    sequence_page_table,
    last_page_fill,
    local_page_ranking,
):
    count_of_rows = queries.shape[0]
    pooled_pages = local_page_ranking.shape[0]
    page_length = key_cache_pages.shape[1]
    query_group_width = QUERY_HEADS // KEY_VALUE_HEADS
    first_page = jnp.cumsum(sequence_page_table) - sequence_page_table
    page_slot = jnp.arange(pooled_pages, dtype=jnp.int32)
    row_ids = jnp.arange(count_of_rows, dtype=jnp.int32)
    inside = (page_slot[:, None] >= first_page[None, :]) & (
        page_slot[:, None] < (first_page + sequence_page_table)[None, :]
    )
    owner_slot = jnp.sum(jnp.where(inside, row_ids[None, :], 0), axis=1)
    index_slot = page_slot - jnp.sum(jnp.where(inside, first_page[None, :], 0), axis=1)
    placed = local_page_ranking[None, :] == page_slot[:, None]
    page_owner = jnp.sum(jnp.where(placed, owner_slot[None, :], 0), axis=1)
    page_index = jnp.sum(jnp.where(placed, index_slot[None, :], 0), axis=1)
    cached = (sequence_page_table - 1) * page_length + last_page_fill
    token_place = (
        page_index[:, None] * page_length + jnp.arange(page_length, dtype=jnp.int32)[None, :]
    )
    visible = (page_owner[None, :, None] == row_ids[:, None, None]) & (
        token_place[None, :, :] < cached[:, None, None]
    )
    visible = visible.reshape(count_of_rows, pooled_pages * page_length)
    score_scale = 1.0 / math.sqrt(HEAD_SIZE)
    query_head_rows = queries.reshape(count_of_rows, KEY_VALUE_HEADS, query_group_width, HEAD_SIZE)
    key_matrix = key_cache_pages.reshape(pooled_pages * page_length, KEY_VALUE_HEADS, HEAD_SIZE)
    value_matrix = value_cache_pages.reshape(pooled_pages * page_length, KEY_VALUE_HEADS, HEAD_SIZE)
    scores = (
        jnp.einsum(
            "rhgd,thd->rhgt", query_head_rows, key_matrix, preferred_element_type=jnp.float32
        )
        * score_scale
    )
    self_score = (
        jnp.einsum(
            "jqnu,jqu->jqn",
            query_head_rows,
            fresh_key_rows.reshape(count_of_rows, KEY_VALUE_HEADS, HEAD_SIZE),
            preferred_element_type=jnp.float32,
        )
        * score_scale
    )
    scores = jnp.where(visible[:, None, None, :], scores, -jnp.inf)
    highest = jnp.maximum(jnp.max(scores, axis=-1), self_score)
    raised = jnp.exp(scores - highest[..., None])
    own_raised = jnp.exp(self_score - highest)
    denominator = jnp.sum(raised, axis=-1) + own_raised
    weights = (raised / denominator[..., None]).astype(jnp.bfloat16)
    self_weight = (own_raised / denominator).astype(jnp.bfloat16)
    mixed_output = jnp.einsum(
        "rhgt,thd->rhgd", weights, value_matrix, preferred_element_type=jnp.float32
    )
    mixed_output = mixed_output + self_weight.astype(jnp.float32)[
        ..., None
    ] * fresh_value_rows.astype(jnp.float32).reshape(count_of_rows, KEY_VALUE_HEADS, 1, HEAD_SIZE)
    return mixed_output.reshape(count_of_rows, QUERY_HEADS * HEAD_SIZE).astype(jnp.bfloat16)


MESH = pl.DeviceIdType.MESH
LANES = 128


def layer_kernel(
    n,
    chunks,
    block_ref,
    residual_ref,
    gain_ref,
    inverse_ref,
    wo_hbm,
    wg_hbm,
    wu_hbm,
    wd_hbm,
    hidden_ref,
    mixture_ref,
    g1,
    g2,
    res,
    wo,
    wg,
    wu,
    wd,
    gate,
    upward,
    squares,
    act,
    part,
    from_core,
    from_y,
    from_z,
    w_sem,
    own_sem,
    send1,
    recv1,
    send2,
    recv2,
    res_send,
    res_recv,
    core_send,
    core_recv,
    y_send,
    y_recv,
    z_send,
    z_recv,
):
    levels = n // 4
    rows = block_ref.shape[0]
    total = n * rows
    cols = residual_ref.shape[2]
    width = D // chunks
    me = lax.axis_index("expert")
    z = lax.div(me, 4)
    y = lax.rem(lax.div(me, 2), 2)
    c = lax.rem(me, 2)
    device = lambda zz, yy, cc: zz * 4 + yy * 2 + cc
    beside_y = device(z, 1 - y, c)
    beside_core = device(z, y, 1 - c)

    weight_copies = [
        pltpu.make_async_copy(source, target, w_sem.at[i])
        for i, (source, target) in enumerate(
            ((wo_hbm, wo), (wg_hbm, wg), (wu_hbm, wu), (wd_hbm, wd))
        )
    ]
    for copy in weight_copies:
        copy.start()

    barrier = pltpu.get_barrier_semaphore()

    @pl.loop(1, n)
    def greet(k):
        pl.semaphore_signal(
            barrier, inc=1, device_id={"expert": lax.rem(me + k, n)}, device_id_type=MESH
        )

    own = pltpu.make_async_copy(block_ref, g1.at[z, y, c], own_sem.at[0])
    own.start()
    own.wait()
    own_res = pltpu.make_async_copy(residual_ref.at[me], res.at[me], own_sem.at[1])
    own_res.start()
    own_res.wait()
    pl.semaphore_wait(barrier, n - 1)

    def gather(buf, send, recv, consume, after_first):
        def copy(zz, yy, cc, way, target):
            return pltpu.make_async_remote_copy(
                src_ref=buf.at[zz, yy, cc],
                dst_ref=buf.at[zz, yy, cc],
                send_sem=send.at[way, zz, yy, cc],
                recv_sem=recv.at[zz, yy, cc],
                device_id={"expert": target},
                device_id_type=MESH,
            )

        def up(zz):
            return copy(zz, y, c, 0, device(jnp.minimum(z + 1, levels - 1), y, c))

        def down(zz):
            return copy(zz, y, c, 1, device(jnp.maximum(z - 1, 0), y, c))

        def across(zz):
            return copy(zz, y, c, 2, beside_y)

        def beside(zz, yy):
            return copy(zz, yy, c, 3, beside_core)

        def landed(zz, yy, cc):
            copy(zz, yy, cc, 3, beside_core).wait_recv()

        def line(zz):
            @pl.when(zz != z)
            def _():
                landed(zz, y, c)

            @pl.when((zz <= z) & (z < levels - 1))
            def _():
                up(zz).start()

            @pl.when((zz >= z) & (z > 0))
            def _():
                down(zz).start()

            across(zz).start()
            beside(zz, y).start()

        def at_distance(distance, body):
            @pl.loop(0, 2)
            def _(sign):
                zz = z - distance + 2 * distance * sign

                @pl.when(
                    (distance >= 0)
                    & (zz >= 0)
                    & (zz < levels)
                    & ((distance > 0) | (sign == 0))
                )
                def _():
                    body(zz)

        def crossed(zz):
            landed(zz, 1 - y, c)
            beside(zz, 1 - y).start()

        @pl.loop(0, levels + 2)
        def step(s):
            at_distance(s, line)
            at_distance(s - 1, crossed)

            @pl.when(s == 0)
            def _():
                after_first()

            if consume is not None:
                at_distance(s, lambda zz: consume(zz, y, c))
                at_distance(s - 1, lambda zz: consume(zz, 1 - y, c))

            def near(zz):
                landed(zz, y, 1 - c)
                if consume is not None:
                    consume(zz, y, 1 - c)

            def far(zz):
                landed(zz, 1 - y, 1 - c)
                if consume is not None:
                    consume(zz, 1 - y, 1 - c)

            at_distance(s - 1, near)
            at_distance(s - 2, far)

        def drain():
            @pl.loop(0, levels)
            def _(zz):
                @pl.when((zz <= z) & (z < levels - 1))
                def _():
                    up(zz).wait_send()

                @pl.when((zz >= z) & (z > 0))
                def _():
                    down(zz).wait_send()

                across(zz).wait_send()
                beside(zz, y).wait_send()
                beside(zz, 1 - y).wait_send()

        return drain

    def residual_copy(k):
        return pltpu.make_async_remote_copy(
            src_ref=residual_ref.at[lax.rem(me + k, n)],
            dst_ref=res.at[me],
            send_sem=res_send.at[k],
            recv_sem=res_recv.at[me],
            device_id={"expert": lax.rem(me + k, n)},
            device_id_type=MESH,
        )

    def residual_landed(k):
        source = lax.rem(me + k, n)
        pltpu.make_async_remote_copy(
            src_ref=residual_ref.at[source],
            dst_ref=res.at[source],
            send_sem=res_send.at[k],
            recv_sem=res_recv.at[source],
            device_id={"expert": source},
            device_id_type=MESH,
        ).wait_recv()

    def send_residual():
        @pl.loop(1, n)
        def _(k):
            residual_copy(k).start()

    drain1 = gather(g1, send1, recv1, None, send_residual)
    weight_copies[0].wait()

    @pl.loop(1, n)
    def _(k):
        residual_landed(k)

    projected = jnp.zeros((total, cols), jnp.float32)
    for k in range(0, D, 1024):
        projected += jnp.dot(
            g1[:, :, :, :, k : k + 1024].reshape(total, 1024),
            wo[k : k + 1024, :],
            preferred_element_type=jnp.float32,
        )
    hidden = res[...].reshape(total, cols).astype(jnp.float32) + projected.astype(
        jnp.bfloat16
    ).astype(jnp.float32)
    g2[z, y, c] = (hidden * gain_ref[me]).astype(jnp.bfloat16)
    gate[...] = jnp.zeros_like(gate)
    upward[...] = jnp.zeros_like(upward)
    squares[...] = jnp.zeros_like(squares)

    def consume(zz, yy, cc):
        d = device(zz, yy, cc)
        block = g2[zz, yy, cc]
        at = pl.ds(pl.multiple_of(d * cols, cols), cols)
        gate[...] += jnp.dot(block, wg[at, :], preferred_element_type=jnp.float32)
        upward[...] += jnp.dot(block, wu[at, :], preferred_element_type=jnp.float32)
        plain = block.astype(jnp.float32) * inverse_ref[d]
        squares[...] += jnp.sum(plain * plain, axis=1, keepdims=True)

    def wait_weights():
        weight_copies[1].wait()
        weight_copies[2].wait()

    drain2 = gather(g2, send2, recv2, consume, wait_weights)
    hidden_ref[...] = g2[:, :, :, pl.ds(pl.multiple_of(me * rows, rows), rows), :].reshape(
        n, rows, cols
    )
    scale = lax.rsqrt(squares[...] * (1.0 / D) + 1e-06)
    gated = gate[...] * scale
    act[...] = (gated / (1.0 + jnp.exp(-gated)) * (upward[...] * scale)).astype(jnp.bfloat16)
    table = g1[:, :, :, :, D : D + LANES].reshape(total, LANES).astype(jnp.float32)
    lane = lax.broadcasted_iota(jnp.int32, (total, LANES), 1)
    table = jnp.where((lane < 3 * levels) & (lax.rem(lane, levels) == z), table, 0.0)
    weight = jnp.sum(table, axis=1, keepdims=True)
    weight_copies[3].wait()

    def core_copy(j):
        return pltpu.make_async_remote_copy(
            src_ref=part.at[j, 1 - c],
            dst_ref=from_core.at[j],
            send_sem=core_send.at[j],
            recv_sem=core_recv.at[j],
            device_id={"expert": beside_core},
            device_id_type=MESH,
        )

    def y_copy(j):
        return pltpu.make_async_remote_copy(
            src_ref=part.at[j, c, 1 - y],
            dst_ref=from_y.at[j],
            send_sem=y_send.at[j],
            recv_sem=y_recv.at[j],
            device_id={"expert": beside_y},
            device_id_type=MESH,
        )

    def z_copy(j, goal, slot, target):
        return pltpu.make_async_remote_copy(
            src_ref=part.at[j, c, y, goal],
            dst_ref=from_z.at[j, slot],
            send_sem=z_send.at[j, goal],
            recv_sem=z_recv.at[j, slot],
            device_id={"expert": target},
            device_id_type=MESH,
        )

    def z_landed(j, slot):
        z_copy(j, 0, slot, beside_y).wait_recv()

    def multiply(j):
        value = jnp.dot(
            act[...],
            wd[:, pl.ds(pl.multiple_of(j * width, width), width)],
            preferred_element_type=jnp.float32,
        )
        value = (value * weight).astype(jnp.bfloat16).reshape(levels, 2, 2, rows, width)
        for yy in range(2):
            for cc in range(2):
                part[j, cc, yy] = value[:, yy, cc]
        core_copy(j).start()

    def add_core(j):
        core_copy(j).wait_recv()
        for yy in range(2):
            part[j, c, yy] = (
                part[j, c, yy].astype(jnp.float32) + from_core[j, yy].astype(jnp.float32)
            ).astype(jnp.bfloat16)
        y_copy(j).start()

    def add_y(j):
        y_copy(j).wait_recv()
        part[j, c, y] = (
            part[j, c, y].astype(jnp.float32) + from_y[j].astype(jnp.float32)
        ).astype(jnp.bfloat16)

    def chain(j, rising):
        count = jnp.where(rising, levels - 1 - z, z)
        first = jnp.where(rising, z == 0, z == levels - 1)
        target = device(jnp.where(rising, z + 1, z - 1), y, c)

        @pl.loop(0, count)
        def _(k):
            goal = jnp.where(rising, levels - 1 - k, k)

            @pl.when(jnp.logical_not(first))
            def _():
                z_landed(j, goal)
                part[j, c, y, goal] = (
                    part[j, c, y, goal].astype(jnp.float32)
                    + from_z[j, goal].astype(jnp.float32)
                ).astype(jnp.bfloat16)

            last_down = jnp.logical_not(rising) & (goal == z - 1)
            z_copy(j, goal, jnp.where(last_down, levels, goal), target).start()

    def chains(j):
        rising = z < levels // 2
        chain(j, rising)
        chain(j, jnp.logical_not(rising))

    def finish(j):
        at = pl.ds(pl.multiple_of(j * width, width), width)
        mixture_ref[:, at] = part[j, c, y, z].astype(jnp.float32)

        @pl.when(z > 0)
        def _():
            z_landed(j, z)
            mixture_ref[:, at] += from_z[j, z].astype(jnp.float32)

        @pl.when(z < levels - 1)
        def _():
            z_landed(j, levels)
            mixture_ref[:, at] += from_z[j, levels].astype(jnp.float32)

    @pl.loop(0, chunks + 1)
    def _(j):
        @pl.when(j < chunks)
        def _():
            multiply(j)

        @pl.when(j > 0)
        def _():
            add_core(j - 1)

    @pl.loop(0, chunks)
    def _(j):
        add_y(j)
        chains(j)

    @pl.loop(0, chunks)
    def _(j):
        finish(j)

    drain1()
    drain2()

    @pl.loop(1, n)
    def _(k):
        residual_copy(k).wait_send()

    @pl.loop(0, chunks)
    def _(j):
        core_copy(j).wait_send()
        y_copy(j).wait_send()

        @pl.loop(0, levels)
        def _(goal):
            @pl.when(goal != z)
            def _():
                z_copy(j, goal, goal, beside_y).wait_send()


def layer(n, block, residual, gain, inverse, wo, wg, wu, wd):
    rows = block.shape[0]
    total = n * rows
    cols = residual.shape[2]
    hidden_units = wg.shape[1]
    levels = n // 4
    chunks = max(4, levels)
    width = D // chunks
    bf16, f32 = jnp.bfloat16, jnp.float32
    vmem = pl.BlockSpec(memory_space=pltpu.VMEM)
    dma = pltpu.SemaphoreType.DMA
    return pl.pallas_call(
        functools.partial(layer_kernel, n, chunks),
        out_shape=(
            jax.ShapeDtypeStruct((n, rows, cols), bf16),
            jax.ShapeDtypeStruct((rows, D), f32),
        ),
        in_specs=[vmem] * 4 + [pl.BlockSpec(memory_space=pl.ANY)] * 4,
        out_specs=(vmem, vmem),
        scratch_shapes=[
            pltpu.VMEM((levels, 2, 2, rows, D + LANES), bf16),
            pltpu.VMEM((levels, 2, 2, total, cols), bf16),
            pltpu.VMEM((n, rows, cols), bf16),
            pltpu.VMEM(wo.shape, bf16),
            pltpu.VMEM(wg.shape, bf16),
            pltpu.VMEM(wu.shape, bf16),
            pltpu.VMEM(wd.shape, bf16),
            pltpu.VMEM((total, hidden_units), f32),
            pltpu.VMEM((total, hidden_units), f32),
            pltpu.VMEM((total, 1), f32),
            pltpu.VMEM((total, hidden_units), bf16),
            pltpu.VMEM((chunks, 2, 2, levels, rows, width), bf16),
            pltpu.VMEM((chunks, 2, levels, rows, width), bf16),
            pltpu.VMEM((chunks, levels, rows, width), bf16),
            pltpu.VMEM((chunks, levels + 1, rows, width), bf16),
            dma((4,)),
            dma((2,)),
            dma((4, levels, 2, 2)),
            dma((levels, 2, 2)),
            dma((4, levels, 2, 2)),
            dma((levels, 2, 2)),
            dma((n,)),
            dma((n,)),
            dma((chunks,)),
            dma((chunks,)),
            dma((chunks,)),
            dma((chunks,)),
            dma((chunks, levels)),
            dma((chunks, levels + 1)),
        ],
        compiler_params=pltpu.CompilerParams(
            collective_id=0, has_side_effects=True, vmem_limit_bytes=62 * 1024 * 1024
        ),
        cost_estimate=pl.CostEstimate(
            flops=2 * total * D * (cols + 3 * hidden_units),
            bytes_accessed=2 * D * (cols + 3 * hidden_units),
            transcendentals=total * hidden_units,
        ),
    )(block, residual, gain, inverse, wo, wg, wu, wd)


def per_device(
    queries,
    fresh_key_rows,
    fresh_value_rows,
    key_cache_pages,
    value_cache_pages,
    sequence_page_table,
    last_page_fill,
    local_page_ranking,
    residual,
    out_weight,
    norm_gain,
    routes,
    route_weight,
    w_gate,
    w_up,
    w_down,
):
    head_out = local_attention(
        queries,
        fresh_key_rows,
        fresh_value_rows,
        key_cache_pages,
        value_cache_pages,
        sequence_page_table[0],
        last_page_fill,
        local_page_ranking[0],
    )
    n = lax.axis_size("expert")
    experts = n // SHARDS
    rows = head_out.shape[0]
    cols = out_weight.shape[1]
    ids = jnp.arange(experts, dtype=jnp.int32)
    table = jnp.sum(
        jnp.where(routes[:, :, None] == ids[None, None, :], route_weight[:, :, None], 0.0), axis=1
    )
    high = lax.reduce_precision(table, 8, 7)
    middle = lax.reduce_precision(table - high, 8, 7)
    low = table - high - middle
    packed = jnp.concatenate([high, middle, low], axis=1).astype(jnp.bfloat16)
    packed = jnp.pad(packed, ((0, 0), (0, LANES - 3 * experts)))
    block = jnp.concatenate([head_out, packed], axis=1)
    gain = norm_gain.astype(jnp.float32)
    inverse = 1.0 / gain
    scaled, mixture = layer(
        n,
        block,
        residual.reshape(rows, n, cols).transpose(1, 0, 2),
        gain.reshape(n, 1, cols),
        inverse.reshape(n, 1, cols),
        out_weight,
        w_gate[0],
        w_up[0],
        w_down[0],
    )
    hidden = scaled.transpose(1, 0, 2).reshape(rows, D).astype(jnp.float32) * inverse
    return (hidden + mixture).astype(jnp.bfloat16)


def solution(mesh):
    return jax.shard_map(
        per_device,
        mesh=mesh,
        in_specs=(
            P(("group", "expert"), None),
            P(("group", "expert"), None),
            P(("group", "expert"), None),
            P(("group", "expert"), None, None),
            P(("group", "expert"), None, None),
            P(("group", "expert"), None),
            P(("group", "expert")),
            P(("group", "expert"), None),
            P(("group", "expert"), None),
            P(None, "expert"),
            P(),
            P(("group", "expert"), None),
            P(("group", "expert"), None),
            P("expert", None, None),
            P("expert", None, None),
            P("expert", None, None),
        ),
        out_specs=P(("group", "expert"), None),
        check_vma=False,
    )
```

```python
import functools
import math

import jax
import jax.numpy as jnp
from jax import lax
from jax.experimental import pallas as pl
from jax.experimental.pallas import tpu as pltpu
from jax.sharding import PartitionSpec as P

D = 4096
QUERY_HEADS = 32
KEY_VALUE_HEADS = 2
HEAD_SIZE = 128


MESH = pl.DeviceIdType.MESH
LANES = 128


def packed_routes(levels, rows, routes_ref, route_weight_ref):
    lane = lax.broadcasted_iota(jnp.int32, (rows, LANES), 1)
    expert = lax.rem(lane, levels)
    table = jnp.zeros((rows, LANES), jnp.float32)
    for t in range(routes_ref.shape[1]):
        table += jnp.where(
            routes_ref[:, t : t + 1] == expert, route_weight_ref[:, t : t + 1], 0.0
        )
    high = table.astype(jnp.bfloat16).astype(jnp.float32)
    middle = (table - high).astype(jnp.bfloat16).astype(jnp.float32)
    low = table - high - middle
    piece = jnp.where(lane < levels, high, jnp.where(lane < 2 * levels, middle, low))
    return jnp.where(lane < 3 * levels, piece, 0.0).astype(jnp.bfloat16)


def attend(
    query_ref,
    fresh_key_ref,
    fresh_value_ref,
    count_ref,
    fill_ref,
    ranking_ref,
    keys,
    values,
    by_head,
    out,
):
    f32 = jnp.float32
    rows = query_ref.shape[0]
    pages, page, _ = keys.shape
    tokens = pages * page
    heads = QUERY_HEADS // KEY_VALUE_HEADS
    group = heads * rows
    iota = lambda shape, axis: lax.broadcasted_iota(jnp.int32, shape, axis)
    diagonal = iota((pages, pages), 0) == iota((pages, pages), 1)
    page_of_slot = jnp.sum(
        jnp.where(diagonal, ranking_ref[...].astype(f32), 0.0), axis=1, keepdims=True
    )
    token = iota((pages, tokens), 1)
    page_of_token = lax.div(token, page).astype(f32)
    slot = jnp.sum(
        jnp.where(page_of_token == page_of_slot, iota((pages, tokens), 0).astype(f32), 0.0),
        axis=0,
        keepdims=True,
    )
    place = slot * page + lax.rem(token[:1], page).astype(f32)
    below = iota((rows, rows), 1) < iota((rows, rows), 0)
    same = iota((rows, rows), 1) == iota((rows, rows), 0)
    counts = count_ref[...].astype(f32)
    lengths = (counts - 1.0) * page + fill_ref[...].astype(f32)
    first = page * jnp.sum(jnp.where(below, counts, 0.0), axis=1, keepdims=True)
    last = first + jnp.sum(jnp.where(same, lengths, 0.0), axis=1, keepdims=True)
    visible = (place >= first) & (place < last)
    bias = jnp.where(visible, 0.0, -jnp.inf)
    scale = 1.0 / math.sqrt(HEAD_SIZE)
    for g in range(KEY_VALUE_HEADS):
        features = slice(g * HEAD_SIZE, (g + 1) * HEAD_SIZE)
        for h in range(heads):
            at = (g * heads + h) * HEAD_SIZE
            by_head[h] = query_ref[:, at : at + HEAD_SIZE]
        query = by_head[...]
        fresh_key = fresh_key_ref[:, features].astype(f32)
        fresh_value = fresh_value_ref[:, features].astype(f32)
        own = scale * jnp.sum(query.astype(f32) * fresh_key[None], axis=2, keepdims=True)
        scores = lax.dot_general(
            query.reshape(group, HEAD_SIZE),
            keys[:, :, features].reshape(tokens, HEAD_SIZE),
            (((1,), (1,)), ((), ())),
            preferred_element_type=f32,
        )
        scores = scores.reshape(heads, rows, tokens) * scale + bias[None]
        highest = jnp.maximum(jnp.max(scores, axis=2, keepdims=True), own)
        raised = jnp.exp(scores - highest)
        own_raised = jnp.exp(own - highest)
        inverse = 1.0 / (jnp.sum(raised, axis=2, keepdims=True) + own_raised)
        mixed = jnp.dot(
            raised.astype(jnp.bfloat16).reshape(group, tokens),
            values[:, :, features].reshape(tokens, HEAD_SIZE),
            preferred_element_type=f32,
        )
        mixed = mixed.reshape(heads, rows, HEAD_SIZE) + own_raised * fresh_value[None]
        mixed = (mixed * inverse).astype(jnp.bfloat16)
        for h in range(heads):
            at = (g * heads + h) * HEAD_SIZE
            out[:, at : at + HEAD_SIZE] = mixed[h]


def layer_kernel(
    n,
    chunks,
    query_ref,
    fresh_key_ref,
    fresh_value_ref,
    count_ref,
    fill_ref,
    ranking_ref,
    residual_ref,
    gain_ref,
    routes_ref,
    route_weight_ref,
    key_hbm,
    value_hbm,
    wo_hbm,
    wg_hbm,
    wu_hbm,
    wd_hbm,
    out_ref,
    keys,
    values,
    by_head,
    residual_out,
    gains,
    inverse,
    hidden_own,
    g1,
    g2,
    res,
    wo,
    wg,
    wu,
    wd,
    gate,
    upward,
    squares,
    act,
    part,
    from_core,
    from_y,
    from_z,
    w_sem,
    send1,
    recv1,
    send2,
    recv2,
    res_send,
    res_recv,
    core_send,
    core_recv,
    y_send,
    y_recv,
    z_send,
    z_recv,
):
    levels = n // 4
    rows = query_ref.shape[0]
    total = n * rows
    cols = D // n
    width = D // chunks
    me = lax.axis_index("expert")
    z = lax.div(me, 4)
    y = lax.rem(lax.div(me, 2), 2)
    c = lax.rem(me, 2)
    device = lambda zz, yy, cc: zz * 4 + yy * 2 + cc
    beside_y = device(z, 1 - y, c)
    beside_core = device(z, y, 1 - c)

    cache_copies = [
        pltpu.make_async_copy(key_hbm, keys, w_sem.at[4]),
        pltpu.make_async_copy(value_hbm, values, w_sem.at[5]),
    ]
    for copy in cache_copies:
        copy.start()
    weight_copies = [
        pltpu.make_async_copy(source, target, w_sem.at[i])
        for i, (source, target) in enumerate(
            ((wo_hbm, wo), (wg_hbm, wg), (wu_hbm, wu), (wd_hbm, wd))
        )
    ]
    for copy in weight_copies:
        copy.start()

    barrier = pltpu.get_barrier_semaphore()

    @pl.loop(1, n)
    def greet(k):
        pl.semaphore_signal(
            barrier, inc=1, device_id={"expert": lax.rem(me + k, n)}, device_id_type=MESH
        )

    for d in range(n):
        at = slice(d * cols, (d + 1) * cols)
        residual_out[d] = residual_ref[:, at]
        gains[d] = gain_ref[:, at].astype(jnp.float32)
        inverse[d] = 1.0 / gains[d]
    res[me] = residual_out[me]
    g1[z, y, c, :, D:] = packed_routes(levels, rows, routes_ref, route_weight_ref)
    for copy in cache_copies:
        copy.wait()
    attend(
        query_ref,
        fresh_key_ref,
        fresh_value_ref,
        count_ref,
        fill_ref,
        ranking_ref,
        keys,
        values,
        by_head,
        g1.at[z, y, c],
    )
    pl.semaphore_wait(barrier, n - 1)

    def gather(buf, send, recv, consume, after_first):
        def copy(zz, yy, cc, way, target):
            return pltpu.make_async_remote_copy(
                src_ref=buf.at[zz, yy, cc],
                dst_ref=buf.at[zz, yy, cc],
                send_sem=send.at[way, zz, yy, cc],
                recv_sem=recv.at[zz, yy, cc],
                device_id={"expert": target},
                device_id_type=MESH,
            )

        def up(zz):
            return copy(zz, y, c, 0, device(jnp.minimum(z + 1, levels - 1), y, c))

        def down(zz):
            return copy(zz, y, c, 1, device(jnp.maximum(z - 1, 0), y, c))

        def across(zz):
            return copy(zz, y, c, 2, beside_y)

        def beside(zz, yy):
            return copy(zz, yy, c, 3, beside_core)

        def landed(zz, yy, cc):
            copy(zz, yy, cc, 3, beside_core).wait_recv()

        def line(zz):
            @pl.when(zz != z)
            def _():
                landed(zz, y, c)

            @pl.when((zz <= z) & (z < levels - 1))
            def _():
                up(zz).start()

            @pl.when((zz >= z) & (z > 0))
            def _():
                down(zz).start()

            across(zz).start()
            beside(zz, y).start()

        def at_distance(distance, body):
            @pl.loop(0, 2)
            def _(sign):
                zz = z - distance + 2 * distance * sign

                @pl.when(
                    (distance >= 0)
                    & (zz >= 0)
                    & (zz < levels)
                    & ((distance > 0) | (sign == 0))
                )
                def _():
                    body(zz)

        def crossed(zz):
            landed(zz, 1 - y, c)
            beside(zz, 1 - y).start()

        @pl.loop(0, levels + 2)
        def step(s):
            at_distance(s, line)
            at_distance(s - 1, crossed)

            @pl.when(s == 0)
            def _():
                after_first()

            if consume is not None:
                at_distance(s, lambda zz: consume(zz, y, c))
                at_distance(s - 1, lambda zz: consume(zz, 1 - y, c))

            def near(zz):
                landed(zz, y, 1 - c)
                if consume is not None:
                    consume(zz, y, 1 - c)

            def far(zz):
                landed(zz, 1 - y, 1 - c)
                if consume is not None:
                    consume(zz, 1 - y, 1 - c)

            at_distance(s - 1, near)
            at_distance(s - 2, far)

        def drain():
            @pl.loop(0, levels)
            def _(zz):
                @pl.when((zz <= z) & (z < levels - 1))
                def _():
                    up(zz).wait_send()

                @pl.when((zz >= z) & (z > 0))
                def _():
                    down(zz).wait_send()

                across(zz).wait_send()
                beside(zz, y).wait_send()
                beside(zz, 1 - y).wait_send()

        return drain

    def residual_copy(k):
        return pltpu.make_async_remote_copy(
            src_ref=residual_out.at[lax.rem(me + k, n)],
            dst_ref=res.at[me],
            send_sem=res_send.at[k],
            recv_sem=res_recv.at[me],
            device_id={"expert": lax.rem(me + k, n)},
            device_id_type=MESH,
        )

    def residual_landed(k):
        source = lax.rem(me + k, n)
        pltpu.make_async_remote_copy(
            src_ref=residual_out.at[source],
            dst_ref=res.at[source],
            send_sem=res_send.at[k],
            recv_sem=res_recv.at[source],
            device_id={"expert": source},
            device_id_type=MESH,
        ).wait_recv()

    def send_residual():
        @pl.loop(1, n)
        def _(k):
            residual_copy(k).start()

    drain1 = gather(g1, send1, recv1, None, send_residual)
    weight_copies[0].wait()

    @pl.loop(1, n)
    def _(k):
        residual_landed(k)

    projected = jnp.zeros((total, cols), jnp.float32)
    for k in range(0, D, 1024):
        projected += jnp.dot(
            g1[:, :, :, :, k : k + 1024].reshape(total, 1024),
            wo[k : k + 1024, :],
            preferred_element_type=jnp.float32,
        )
    hidden = res[...].reshape(total, cols).astype(jnp.float32) + projected.astype(
        jnp.bfloat16
    ).astype(jnp.float32)
    g2[z, y, c] = (hidden * gains[me]).astype(jnp.bfloat16)
    gate[...] = jnp.zeros_like(gate)
    upward[...] = jnp.zeros_like(upward)
    squares[...] = jnp.zeros_like(squares)

    def consume(zz, yy, cc):
        d = device(zz, yy, cc)
        block = g2[zz, yy, cc]
        at = pl.ds(pl.multiple_of(d * cols, cols), cols)
        gate[...] += jnp.dot(block, wg[at, :], preferred_element_type=jnp.float32)
        upward[...] += jnp.dot(block, wu[at, :], preferred_element_type=jnp.float32)
        plain = block.astype(jnp.float32) * inverse[d]
        squares[...] += jnp.sum(plain * plain, axis=1, keepdims=True)

    def wait_weights():
        weight_copies[1].wait()
        weight_copies[2].wait()

    drain2 = gather(g2, send2, recv2, consume, wait_weights)
    scale = lax.rsqrt(squares[...] * (1.0 / D) + 1e-06)
    gated = gate[...] * scale
    act[...] = (gated / (1.0 + jnp.exp(-gated)) * (upward[...] * scale)).astype(jnp.bfloat16)
    table = g1[:, :, :, :, D : D + LANES].reshape(total, LANES).astype(jnp.float32)
    lane = lax.broadcasted_iota(jnp.int32, (total, LANES), 1)
    table = jnp.where((lane < 3 * levels) & (lax.rem(lane, levels) == z), table, 0.0)
    weight = jnp.sum(table, axis=1, keepdims=True)
    weight_copies[3].wait()

    def core_copy(j):
        return pltpu.make_async_remote_copy(
            src_ref=part.at[j, 1 - c],
            dst_ref=from_core.at[j],
            send_sem=core_send.at[j],
            recv_sem=core_recv.at[j],
            device_id={"expert": beside_core},
            device_id_type=MESH,
        )

    def y_copy(j):
        return pltpu.make_async_remote_copy(
            src_ref=part.at[j, c, 1 - y],
            dst_ref=from_y.at[j],
            send_sem=y_send.at[j],
            recv_sem=y_recv.at[j],
            device_id={"expert": beside_y},
            device_id_type=MESH,
        )

    def z_copy(j, goal, slot, target):
        return pltpu.make_async_remote_copy(
            src_ref=part.at[j, c, y, goal],
            dst_ref=from_z.at[j, slot],
            send_sem=z_send.at[j, goal],
            recv_sem=z_recv.at[j, slot],
            device_id={"expert": target},
            device_id_type=MESH,
        )

    def z_landed(j, slot):
        z_copy(j, 0, slot, beside_y).wait_recv()

    def multiply(j):
        value = jnp.dot(
            act[...],
            wd[:, pl.ds(pl.multiple_of(j * width, width), width)],
            preferred_element_type=jnp.float32,
        )
        value = (value * weight).astype(jnp.bfloat16).reshape(levels, 2, 2, rows, width)
        for yy in range(2):
            for cc in range(2):
                part[j, cc, yy] = value[:, yy, cc]
        core_copy(j).start()

    def add_core(j):
        core_copy(j).wait_recv()
        for yy in range(2):
            part[j, c, yy] = (
                part[j, c, yy].astype(jnp.float32) + from_core[j, yy].astype(jnp.float32)
            ).astype(jnp.bfloat16)
        y_copy(j).start()

    def add_y(j):
        y_copy(j).wait_recv()
        part[j, c, y] = (
            part[j, c, y].astype(jnp.float32) + from_y[j].astype(jnp.float32)
        ).astype(jnp.bfloat16)

    def chain(j, rising):
        count = jnp.where(rising, levels - 1 - z, z)
        first = jnp.where(rising, z == 0, z == levels - 1)
        target = device(jnp.where(rising, z + 1, z - 1), y, c)

        @pl.loop(0, count)
        def _(k):
            goal = jnp.where(rising, levels - 1 - k, k)

            @pl.when(jnp.logical_not(first))
            def _():
                z_landed(j, goal)
                part[j, c, y, goal] = (
                    part[j, c, y, goal].astype(jnp.float32)
                    + from_z[j, goal].astype(jnp.float32)
                ).astype(jnp.bfloat16)

            last_down = jnp.logical_not(rising) & (goal == z - 1)
            z_copy(j, goal, jnp.where(last_down, levels, goal), target).start()

    def chains(j):
        rising = z < levels // 2
        chain(j, rising)
        chain(j, jnp.logical_not(rising))

    def finish(j):
        at = pl.ds(pl.multiple_of(j * width, width), width)
        hidden_own[:, at] += part[j, c, y, z].astype(jnp.float32)

        @pl.when(z > 0)
        def _():
            z_landed(j, z)
            hidden_own[:, at] += from_z[j, z].astype(jnp.float32)

        @pl.when(z < levels - 1)
        def _():
            z_landed(j, levels)
            hidden_own[:, at] += from_z[j, levels].astype(jnp.float32)

        out_ref[:, at] = hidden_own[:, at].astype(jnp.bfloat16)

    @pl.loop(0, chunks + 1)
    def _(j):
        @pl.when(j < chunks)
        def _():
            multiply(j)

        @pl.when(j > 0)
        def _():
            add_core(j - 1)

    for d in range(n):
        mine = g2[d // 4, d // 2 % 2, d % 2, pl.ds(pl.multiple_of(me * rows, rows), rows), :]
        hidden_own[:, d * cols : (d + 1) * cols] = mine.astype(jnp.float32) * inverse[d]

    @pl.loop(0, chunks)
    def _(j):
        add_y(j)
        chains(j)

    @pl.loop(0, chunks)
    def _(j):
        finish(j)

    drain1()
    drain2()

    @pl.loop(1, n)
    def _(k):
        residual_copy(k).wait_send()

    @pl.loop(0, chunks)
    def _(j):
        core_copy(j).wait_send()
        y_copy(j).wait_send()

        @pl.loop(0, levels)
        def _(goal):
            @pl.when(goal != z)
            def _():
                z_copy(j, goal, goal, beside_y).wait_send()


def layer(n, *operands):
    queries, keys, wo, wg, wu, wd = operands[0], operands[10], *operands[12:]
    rows = queries.shape[0]
    total = n * rows
    cols = wo.shape[1]
    hidden_units = wg.shape[1]
    levels = n // 4
    chunks = max(4, levels)
    width = D // chunks
    bf16, f32 = jnp.bfloat16, jnp.float32
    vmem = pl.BlockSpec(memory_space=pltpu.VMEM)
    dma = pltpu.SemaphoreType.DMA
    return pl.pallas_call(
        functools.partial(layer_kernel, n, chunks),
        out_shape=jax.ShapeDtypeStruct((rows, D), bf16),
        in_specs=[vmem] * 10 + [pl.BlockSpec(memory_space=pl.ANY)] * 6,
        out_specs=vmem,
        scratch_shapes=[
            pltpu.VMEM(keys.shape, bf16),
            pltpu.VMEM(keys.shape, bf16),
            pltpu.VMEM((QUERY_HEADS // KEY_VALUE_HEADS, rows, HEAD_SIZE), bf16),
            pltpu.VMEM((n, rows, cols), bf16),
            pltpu.VMEM((n, 1, cols), f32),
            pltpu.VMEM((n, 1, cols), f32),
            pltpu.VMEM((rows, D), f32),
            pltpu.VMEM((levels, 2, 2, rows, D + LANES), bf16),
            pltpu.VMEM((levels, 2, 2, total, cols), bf16),
            pltpu.VMEM((n, rows, cols), bf16),
            pltpu.VMEM(wo.shape, bf16),
            pltpu.VMEM(wg.shape, bf16),
            pltpu.VMEM(wu.shape, bf16),
            pltpu.VMEM(wd.shape, bf16),
            pltpu.VMEM((total, hidden_units), f32),
            pltpu.VMEM((total, hidden_units), f32),
            pltpu.VMEM((total, 1), f32),
            pltpu.VMEM((total, hidden_units), bf16),
            pltpu.VMEM((chunks, 2, 2, levels, rows, width), bf16),
            pltpu.VMEM((chunks, 2, levels, rows, width), bf16),
            pltpu.VMEM((chunks, levels, rows, width), bf16),
            pltpu.VMEM((chunks, levels + 1, rows, width), bf16),
            dma((6,)),
            dma((4, levels, 2, 2)),
            dma((levels, 2, 2)),
            dma((4, levels, 2, 2)),
            dma((levels, 2, 2)),
            dma((n,)),
            dma((n,)),
            dma((chunks,)),
            dma((chunks,)),
            dma((chunks,)),
            dma((chunks,)),
            dma((chunks, levels)),
            dma((chunks, levels + 1)),
        ],
        compiler_params=pltpu.CompilerParams(
            collective_id=0, has_side_effects=True, vmem_limit_bytes=62 * 1024 * 1024
        ),
        cost_estimate=pl.CostEstimate(
            flops=2 * total * D * (cols + 3 * hidden_units),
            bytes_accessed=2 * D * (cols + 3 * hidden_units),
            transcendentals=total * hidden_units,
        ),
    )(*operands)


def per_device(
    queries,
    fresh_key_rows,
    fresh_value_rows,
    key_cache_pages,
    value_cache_pages,
    sequence_page_table,
    last_page_fill,
    local_page_ranking,
    residual,
    out_weight,
    norm_gain,
    routes,
    route_weight,
    w_gate,
    w_up,
    w_down,
):
    return layer(
        lax.axis_size("expert"),
        queries,
        fresh_key_rows,
        fresh_value_rows,
        sequence_page_table,
        last_page_fill.reshape(1, -1),
        local_page_ranking,
        residual,
        norm_gain.reshape(1, -1),
        routes,
        route_weight,
        key_cache_pages,
        value_cache_pages,
        out_weight,
        w_gate[0],
        w_up[0],
        w_down[0],
    )


def solution(mesh):
    return jax.shard_map(
        per_device,
        mesh=mesh,
        in_specs=(
            P(("group", "expert"), None),
            P(("group", "expert"), None),
            P(("group", "expert"), None),
            P(("group", "expert"), None, None),
            P(("group", "expert"), None, None),
            P(("group", "expert"), None),
            P(("group", "expert")),
            P(("group", "expert"), None),
            P(("group", "expert"), None),
            P(None, "expert"),
            P(),
            P(("group", "expert"), None),
            P(("group", "expert"), None),
            P("expert", None, None),
            P("expert", None, None),
            P("expert", None, None),
        ),
        out_specs=P(("group", "expert"), None),
        check_vma=False,
    )
```

```python
import functools
import math

import jax
import jax.numpy as jnp
from jax import lax
from jax.experimental import pallas as pl
from jax.experimental.pallas import tpu as pltpu
from jax.sharding import PartitionSpec as P

D = 4096
QUERY_HEADS = 32
KEY_VALUE_HEADS = 2
HEAD_SIZE = 128


MESH = pl.DeviceIdType.MESH
LANES = 128


def packed_routes(levels, rows, routes_ref, route_weight_ref):
    lane = lax.broadcasted_iota(jnp.int32, (rows, LANES), 1)
    expert = lax.rem(lane, levels)
    table = jnp.zeros((rows, LANES), jnp.float32)
    same = lax.broadcasted_iota(jnp.int32, (rows, rows), 0) == lax.broadcasted_iota(
        jnp.int32, (rows, rows), 1
    )
    upright = lambda line: jnp.sum(jnp.where(same, line, 0.0), axis=1, keepdims=True)
    for t in range(routes_ref.shape[0]):
        route = upright(routes_ref[t : t + 1, :].astype(jnp.float32))
        weight = upright(route_weight_ref[t : t + 1, :])
        table += jnp.where(route == expert.astype(jnp.float32), weight, 0.0)
    high = table.astype(jnp.bfloat16).astype(jnp.float32)
    middle = (table - high).astype(jnp.bfloat16).astype(jnp.float32)
    low = table - high - middle
    piece = jnp.where(lane < levels, high, jnp.where(lane < 2 * levels, middle, low))
    return jnp.where(lane < 3 * levels, piece, 0.0).astype(jnp.bfloat16)


def attend(
    query_ref,
    fresh_key_ref,
    fresh_value_ref,
    count_ref,
    fill_ref,
    ranking_ref,
    keys,
    values,
    by_head,
    out,
    finished,
):
    f32 = jnp.float32
    rows = query_ref.shape[0]
    pages, page, _ = keys.shape
    tokens = pages * page
    heads = QUERY_HEADS // KEY_VALUE_HEADS
    group = heads * rows
    iota = lambda shape, axis: lax.broadcasted_iota(jnp.int32, shape, axis)
    diagonal = iota((pages, pages), 0) == iota((pages, pages), 1)
    page_of_slot = jnp.sum(
        jnp.where(diagonal, ranking_ref[...].astype(f32), 0.0), axis=1, keepdims=True
    )
    token = iota((pages, tokens), 1)
    page_of_token = lax.div(token, page).astype(f32)
    slot = jnp.sum(
        jnp.where(page_of_token == page_of_slot, iota((pages, tokens), 0).astype(f32), 0.0),
        axis=0,
        keepdims=True,
    )
    place = slot * page + lax.rem(token[:1], page).astype(f32)
    below = iota((rows, rows), 1) < iota((rows, rows), 0)
    same = iota((rows, rows), 1) == iota((rows, rows), 0)
    counts = count_ref[...].astype(f32)
    lengths = (counts - 1.0) * page + fill_ref[...].astype(f32)
    first = page * jnp.sum(jnp.where(below, counts, 0.0), axis=1, keepdims=True)
    last = first + jnp.sum(jnp.where(same, lengths, 0.0), axis=1, keepdims=True)
    visible = (place >= first) & (place < last)
    bias = jnp.where(visible, 0.0, -jnp.inf)
    scale = 1.0 / math.sqrt(HEAD_SIZE)
    for g in range(KEY_VALUE_HEADS):
        features = slice(g * HEAD_SIZE, (g + 1) * HEAD_SIZE)
        for h in range(heads):
            at = (g * heads + h) * HEAD_SIZE
            by_head[h] = query_ref[:, at : at + HEAD_SIZE]
        query = by_head[...]
        fresh_key = fresh_key_ref[:, features].astype(f32)
        fresh_value = fresh_value_ref[:, features].astype(f32)
        own = scale * jnp.sum(query.astype(f32) * fresh_key[None], axis=2, keepdims=True)
        scores = lax.dot_general(
            query.reshape(group, HEAD_SIZE),
            keys[:, :, features].reshape(tokens, HEAD_SIZE),
            (((1,), (1,)), ((), ())),
            preferred_element_type=f32,
        )
        scores = scores.reshape(heads, rows, tokens) * scale + bias[None]
        highest = jnp.maximum(jnp.max(scores, axis=2, keepdims=True), own)
        raised = jnp.exp(scores - highest)
        own_raised = jnp.exp(own - highest)
        inverse = 1.0 / (jnp.sum(raised, axis=2, keepdims=True) + own_raised)
        mixed = jnp.dot(
            raised.astype(jnp.bfloat16).reshape(group, tokens),
            values[:, :, features].reshape(tokens, HEAD_SIZE),
            preferred_element_type=f32,
        )
        mixed = mixed.reshape(heads, rows, HEAD_SIZE) + own_raised * fresh_value[None]
        mixed = (mixed * inverse).astype(jnp.bfloat16)
        for h in range(heads):
            at = (g * heads + h) * HEAD_SIZE
            out[:, at : at + HEAD_SIZE] = mixed[h]
        finished(g)


def layer_kernel(
    n,
    chunks,
    query_ref,
    fresh_key_ref,
    fresh_value_ref,
    count_ref,
    fill_ref,
    ranking_ref,
    residual_ref,
    gain_ref,
    routes_ref,
    route_weight_ref,
    key_hbm,
    value_hbm,
    wo_hbm,
    wg_hbm,
    wu_hbm,
    wd_hbm,
    out_ref,
    keys,
    values,
    by_head,
    residual_out,
    gains,
    inverse,
    hidden_own,
    g1,
    g2,
    res,
    wo,
    wg,
    wu,
    wd,
    gate,
    upward,
    squares,
    act,
    part,
    from_core,
    from_y,
    from_z,
    w_sem,
    send1,
    recv1,
    send2,
    recv2,
    res_send,
    res_recv,
    core_send,
    core_recv,
    y_send,
    y_recv,
    z_send,
    z_recv,
):
    levels = n // 4
    rows = query_ref.shape[0]
    total = n * rows
    cols = D // n
    width = D // chunks
    me = lax.axis_index("expert")
    z = lax.div(me, 4)
    y = lax.rem(lax.div(me, 2), 2)
    c = lax.rem(me, 2)
    device = lambda zz, yy, cc: zz * 4 + yy * 2 + cc
    beside_y = device(z, 1 - y, c)
    beside_core = device(z, y, 1 - c)

    cache_copies = [
        pltpu.make_async_copy(key_hbm, keys, w_sem.at[4]),
        pltpu.make_async_copy(value_hbm, values, w_sem.at[5]),
    ]
    for copy in cache_copies:
        copy.start()
    weight_copies = [
        pltpu.make_async_copy(source, target, w_sem.at[i])
        for i, (source, target) in enumerate(
            ((wo_hbm, wo), (wg_hbm, wg), (wu_hbm, wu), (wd_hbm, wd))
        )
    ]
    for copy in weight_copies:
        copy.start()

    barrier = pltpu.get_barrier_semaphore()

    @pl.loop(1, n)
    def greet(k):
        pl.semaphore_signal(
            barrier, inc=1, device_id={"expert": lax.rem(me + k, n)}, device_id_type=MESH
        )

    def gather(buf, send, recv, slices, consume):
        pieces = range(len(slices))

        def copy(p, zz, yy, cc, way, target):
            return pltpu.make_async_remote_copy(
                src_ref=buf.at[(zz, yy, cc) + slices[p]],
                dst_ref=buf.at[(zz, yy, cc) + slices[p]],
                send_sem=send.at[p, way, zz, yy, cc],
                recv_sem=recv.at[p, zz, yy, cc],
                device_id={"expert": target},
                device_id_type=MESH,
            )

        def up(p, zz):
            return copy(p, zz, y, c, 0, device(jnp.minimum(z + 1, levels - 1), y, c))

        def down(p, zz):
            return copy(p, zz, y, c, 1, device(jnp.maximum(z - 1, 0), y, c))

        def across(p, zz):
            return copy(p, zz, y, c, 2, beside_y)

        def beside(p, zz, yy):
            return copy(p, zz, yy, c, 3, beside_core)

        def landed(p, zz, yy, cc):
            copy(p, zz, yy, cc, 3, beside_core).wait_recv()

        def line(p, zz):
            @pl.when((zz <= z) & (z < levels - 1))
            def _():
                up(p, zz).start()

            @pl.when((zz >= z) & (z > 0))
            def _():
                down(p, zz).start()

            across(p, zz).start()
            beside(p, zz, y).start()

        def along(p, zz):
            landed(p, zz, y, c)
            line(p, zz)

        def crossed(p, zz):
            landed(p, zz, 1 - y, c)
            beside(p, zz, 1 - y).start()

        def at_distance(distance, body):
            @pl.loop(0, 2)
            def _(sign):
                zz = z - distance + 2 * distance * sign

                @pl.when(
                    (distance >= 0)
                    & (zz >= 0)
                    & (zz < levels)
                    & ((distance > 0) | (sign == 0))
                )
                def _():
                    body(zz)

        def start(p):
            line(p, z)

        def relay():
            if consume is not None:
                consume(z, y, c)

            @pl.loop(1, levels + 2)
            def step(s):
                for p in pieces:
                    at_distance(s, functools.partial(along, p))
                    at_distance(s - 1, functools.partial(crossed, p))
                if consume is not None:
                    at_distance(s, lambda zz: consume(zz, y, c))
                    at_distance(s - 1, lambda zz: consume(zz, 1 - y, c))

                def arrived(zz, yy):
                    for p in pieces:
                        landed(p, zz, yy, 1 - c)
                    if consume is not None:
                        consume(zz, yy, 1 - c)

                at_distance(s - 1, lambda zz: arrived(zz, y))
                at_distance(s - 2, lambda zz: arrived(zz, 1 - y))

        def drain():
            @pl.loop(0, levels)
            def _(zz):
                for p in pieces:

                    @pl.when((zz <= z) & (z < levels - 1))
                    def _():
                        up(p, zz).wait_send()

                    @pl.when((zz >= z) & (z > 0))
                    def _():
                        down(p, zz).wait_send()

                    across(p, zz).wait_send()
                    beside(p, zz, y).wait_send()
                    beside(p, zz, 1 - y).wait_send()

        return start, relay, drain

    quarter = D // 4
    columns = [(slice(None), pl.ds(p * quarter, quarter)) for p in range(3)]
    columns.append((slice(None), pl.ds(3 * quarter, quarter + LANES)))
    start1, relay1, drain1 = gather(g1, send1, recv1, columns, None)

    def finished(g):
        if g == 0:
            pl.semaphore_wait(barrier, n - 1)
        start1(2 * g)
        start1(2 * g + 1)

    for d in range(n):
        at = slice(d * cols, (d + 1) * cols)
        residual_out[d] = residual_ref[:, at]
        gains[d] = gain_ref[at].astype(jnp.float32).reshape(1, cols)
        inverse[d] = 1.0 / gains[d]
    res[me] = residual_out[me]
    g1[z, y, c, :, D:] = packed_routes(levels, rows, routes_ref, route_weight_ref)
    for copy in cache_copies:
        copy.wait()
    attend(
        query_ref,
        fresh_key_ref,
        fresh_value_ref,
        count_ref,
        fill_ref,
        ranking_ref,
        keys,
        values,
        by_head,
        g1.at[z, y, c],
        finished,
    )

    def residual_copy(k):
        return pltpu.make_async_remote_copy(
            src_ref=residual_out.at[lax.rem(me + k, n)],
            dst_ref=res.at[me],
            send_sem=res_send.at[k],
            recv_sem=res_recv.at[me],
            device_id={"expert": lax.rem(me + k, n)},
            device_id_type=MESH,
        )

    def residual_landed(k):
        source = lax.rem(me + k, n)
        pltpu.make_async_remote_copy(
            src_ref=residual_out.at[source],
            dst_ref=res.at[source],
            send_sem=res_send.at[k],
            recv_sem=res_recv.at[source],
            device_id={"expert": source},
            device_id_type=MESH,
        ).wait_recv()

    @pl.loop(1, n)
    def _(k):
        residual_copy(k).start()

    relay1()
    weight_copies[0].wait()

    @pl.loop(1, n)
    def _(k):
        residual_landed(k)

    projected = jnp.zeros((total, cols), jnp.float32)
    for k in range(0, D, 1024):
        projected += jnp.dot(
            g1[:, :, :, :, k : k + 1024].reshape(total, 1024),
            wo[k : k + 1024, :],
            preferred_element_type=jnp.float32,
        )
    hidden = res[...].reshape(total, cols).astype(jnp.float32) + projected.astype(
        jnp.bfloat16
    ).astype(jnp.float32)
    g2[z, y, c] = (hidden * gains[me]).astype(jnp.bfloat16)
    gate[...] = jnp.zeros_like(gate)
    upward[...] = jnp.zeros_like(upward)
    squares[...] = jnp.zeros_like(squares)

    def consume(zz, yy, cc):
        d = device(zz, yy, cc)
        block = g2[zz, yy, cc]
        at = pl.ds(pl.multiple_of(d * cols, cols), cols)
        gate[...] += jnp.dot(block, wg[at, :], preferred_element_type=jnp.float32)
        upward[...] += jnp.dot(block, wu[at, :], preferred_element_type=jnp.float32)
        plain = block.astype(jnp.float32) * inverse[d]
        squares[...] += jnp.sum(plain * plain, axis=1, keepdims=True)

    share = total // 4
    strips = [(pl.ds(p * share, share), slice(None)) for p in range(4)]
    start2, relay2, drain2 = gather(g2, send2, recv2, strips, consume)
    for p in range(4):
        start2(p)
    weight_copies[1].wait()
    weight_copies[2].wait()
    relay2()
    scale = lax.rsqrt(squares[...] * (1.0 / D) + 1e-06)
    gated = gate[...] * scale
    act[...] = (gated / (1.0 + jnp.exp(-gated)) * (upward[...] * scale)).astype(jnp.bfloat16)
    table = g1[:, :, :, :, D : D + LANES].reshape(total, LANES).astype(jnp.float32)
    lane = lax.broadcasted_iota(jnp.int32, (total, LANES), 1)
    table = jnp.where((lane < 3 * levels) & (lax.rem(lane, levels) == z), table, 0.0)
    weight = jnp.sum(table, axis=1, keepdims=True)
    weight_copies[3].wait()

    def core_copy(j):
        return pltpu.make_async_remote_copy(
            src_ref=part.at[j, 1 - c],
            dst_ref=from_core.at[j],
            send_sem=core_send.at[j],
            recv_sem=core_recv.at[j],
            device_id={"expert": beside_core},
            device_id_type=MESH,
        )

    def y_copy(j):
        return pltpu.make_async_remote_copy(
            src_ref=part.at[j, c, 1 - y],
            dst_ref=from_y.at[j],
            send_sem=y_send.at[j],
            recv_sem=y_recv.at[j],
            device_id={"expert": beside_y},
            device_id_type=MESH,
        )

    def z_copy(j, goal):
        return pltpu.make_async_remote_copy(
            src_ref=part.at[j, c, y, goal],
            dst_ref=from_z.at[j, z],
            send_sem=z_send.at[j, goal],
            recv_sem=z_recv.at[j, z],
            device_id={"expert": device(goal, y, c)},
            device_id_type=MESH,
        )

    def z_landed(j, source):
        pltpu.make_async_remote_copy(
            src_ref=part.at[j, c, y, source],
            dst_ref=from_z.at[j, source],
            send_sem=z_send.at[j, source],
            recv_sem=z_recv.at[j, source],
            device_id={"expert": device(source, y, c)},
            device_id_type=MESH,
        ).wait_recv()

    def multiply(j):
        value = jnp.dot(
            act[...],
            wd[:, pl.ds(pl.multiple_of(j * width, width), width)],
            preferred_element_type=jnp.float32,
        )
        value = (value * weight).astype(jnp.bfloat16).reshape(levels, 2, 2, rows, width)
        for yy in range(2):
            for cc in range(2):
                part[j, cc, yy] = value[:, yy, cc]
        core_copy(j).start()

    def add_core(j):
        core_copy(j).wait_recv()
        for yy in range(2):
            part[j, c, yy] = (
                part[j, c, yy].astype(jnp.float32) + from_core[j, yy].astype(jnp.float32)
            ).astype(jnp.bfloat16)
        y_copy(j).start()

    def add_y(j):
        y_copy(j).wait_recv()
        part[j, c, y] = (
            part[j, c, y].astype(jnp.float32) + from_y[j].astype(jnp.float32)
        ).astype(jnp.bfloat16)

    def scatter(j):
        @pl.loop(1, levels)
        def _(k):
            z_copy(j, lax.rem(z + k, levels)).start()

    def finish(j):
        at = pl.ds(pl.multiple_of(j * width, width), width)
        hidden_own[:, at] += part[j, c, y, z].astype(jnp.float32)

        @pl.loop(1, levels)
        def _(k):
            source = lax.rem(z + k, levels)
            z_landed(j, source)
            hidden_own[:, at] += from_z[j, source].astype(jnp.float32)

        out_ref[:, at] = hidden_own[:, at].astype(jnp.bfloat16)

    @pl.loop(0, chunks + 1)
    def _(j):
        @pl.when(j < chunks)
        def _():
            multiply(j)

        @pl.when(j > 0)
        def _():
            add_core(j - 1)

    for d in range(n):
        mine = g2[d // 4, d // 2 % 2, d % 2, pl.ds(pl.multiple_of(me * rows, rows), rows), :]
        hidden_own[:, d * cols : (d + 1) * cols] = mine.astype(jnp.float32) * inverse[d]

    @pl.loop(0, chunks)
    def _(j):
        add_y(j)
        scatter(j)

    @pl.loop(0, chunks)
    def _(j):
        finish(j)

    drain1()
    drain2()

    @pl.loop(1, n)
    def _(k):
        residual_copy(k).wait_send()

    @pl.loop(0, chunks)
    def _(j):
        core_copy(j).wait_send()
        y_copy(j).wait_send()

        @pl.loop(0, levels)
        def _(goal):
            @pl.when(goal != z)
            def _():
                z_copy(j, goal).wait_send()


def layer(n, *operands):
    queries, keys, wo, wg, wu, wd = operands[0], operands[10], *operands[12:]
    rows = queries.shape[0]
    total = n * rows
    cols = wo.shape[1]
    hidden_units = wg.shape[1]
    levels = n // 4
    chunks = max(4, levels)
    width = D // chunks
    bf16, f32 = jnp.bfloat16, jnp.float32
    vmem = pl.BlockSpec(memory_space=pltpu.VMEM)
    dma = pltpu.SemaphoreType.DMA
    return pl.pallas_call(
        functools.partial(layer_kernel, n, chunks),
        out_shape=jax.ShapeDtypeStruct((rows, D), bf16),
        in_specs=[vmem] * 10 + [pl.BlockSpec(memory_space=pl.ANY)] * 6,
        out_specs=vmem,
        scratch_shapes=[
            pltpu.VMEM(keys.shape, bf16),
            pltpu.VMEM(keys.shape, bf16),
            pltpu.VMEM((QUERY_HEADS // KEY_VALUE_HEADS, rows, HEAD_SIZE), bf16),
            pltpu.VMEM((n, rows, cols), bf16),
            pltpu.VMEM((n, 1, cols), f32),
            pltpu.VMEM((n, 1, cols), f32),
            pltpu.VMEM((rows, D), f32),
            pltpu.VMEM((levels, 2, 2, rows, D + LANES), bf16),
            pltpu.VMEM((levels, 2, 2, total, cols), bf16),
            pltpu.VMEM((n, rows, cols), bf16),
            pltpu.VMEM(wo.shape, bf16),
            pltpu.VMEM(wg.shape, bf16),
            pltpu.VMEM(wu.shape, bf16),
            pltpu.VMEM(wd.shape, bf16),
            pltpu.VMEM((total, hidden_units), f32),
            pltpu.VMEM((total, hidden_units), f32),
            pltpu.VMEM((total, 1), f32),
            pltpu.VMEM((total, hidden_units), bf16),
            pltpu.VMEM((chunks, 2, 2, levels, rows, width), bf16),
            pltpu.VMEM((chunks, 2, levels, rows, width), bf16),
            pltpu.VMEM((chunks, levels, rows, width), bf16),
            pltpu.VMEM((chunks, levels, rows, width), bf16),
            dma((6,)),
            dma((4, 4, levels, 2, 2)),
            dma((4, levels, 2, 2)),
            dma((4, 4, levels, 2, 2)),
            dma((4, levels, 2, 2)),
            dma((n,)),
            dma((n,)),
            dma((chunks,)),
            dma((chunks,)),
            dma((chunks,)),
            dma((chunks,)),
            dma((chunks, levels)),
            dma((chunks, levels)),
        ],
        compiler_params=pltpu.CompilerParams(
            collective_id=0, has_side_effects=True, vmem_limit_bytes=62 * 1024 * 1024
        ),
        cost_estimate=pl.CostEstimate(
            flops=2 * total * D * (cols + 3 * hidden_units),
            bytes_accessed=2 * D * (cols + 3 * hidden_units),
            transcendentals=total * hidden_units,
        ),
    )(*operands)


def per_device(
    queries,
    fresh_key_rows,
    fresh_value_rows,
    key_cache_pages,
    value_cache_pages,
    sequence_page_table,
    last_page_fill,
    local_page_ranking,
    residual,
    out_weight,
    norm_gain,
    routes,
    route_weight,
    w_gate,
    w_up,
    w_down,
):
    return layer(
        lax.axis_size("expert"),
        queries,
        fresh_key_rows,
        fresh_value_rows,
        sequence_page_table,
        last_page_fill.reshape(1, -1),
        local_page_ranking,
        residual,
        norm_gain,
        routes.T,
        route_weight.T,
        key_cache_pages,
        value_cache_pages,
        out_weight,
        w_gate[0],
        w_up[0],
        w_down[0],
    )


def solution(mesh):
    return jax.shard_map(
        per_device,
        mesh=mesh,
        in_specs=(
            P(("group", "expert"), None),
            P(("group", "expert"), None),
            P(("group", "expert"), None),
            P(("group", "expert"), None, None),
            P(("group", "expert"), None, None),
            P(("group", "expert"), None),
            P(("group", "expert")),
            P(("group", "expert"), None),
            P(("group", "expert"), None),
            P(None, "expert"),
            P(),
            P(("group", "expert"), None),
            P(("group", "expert"), None),
            P("expert", None, None),
            P("expert", None, None),
            P("expert", None, None),
        ),
        out_specs=P(("group", "expert"), None),
        check_vma=False,
    )
```

```python
import functools
import math

import jax
import jax.numpy as jnp
from jax import lax
from jax.experimental import pallas as pl
from jax.experimental.pallas import tpu as pltpu
from jax.sharding import PartitionSpec as P

D = 4096
QUERY_HEADS = 32
KEY_VALUE_HEADS = 2
HEAD_SIZE = 128


MESH = pl.DeviceIdType.MESH
LANES = 128


def packed_routes(levels, rows, routes_ref, route_weight_ref):
    lane = lax.broadcasted_iota(jnp.int32, (rows, LANES), 1)
    expert = lax.rem(lane, levels)
    table = jnp.zeros((rows, LANES), jnp.float32)
    same = lax.broadcasted_iota(jnp.int32, (rows, rows), 0) == lax.broadcasted_iota(
        jnp.int32, (rows, rows), 1
    )
    upright = lambda line: jnp.sum(jnp.where(same, line, 0.0), axis=1, keepdims=True)
    for t in range(routes_ref.shape[0]):
        route = upright(routes_ref[t : t + 1, :].astype(jnp.float32))
        weight = upright(route_weight_ref[t : t + 1, :])
        table += jnp.where(route == expert.astype(jnp.float32), weight, 0.0)
    high = table.astype(jnp.bfloat16).astype(jnp.float32)
    middle = (table - high).astype(jnp.bfloat16).astype(jnp.float32)
    low = table - high - middle
    piece = jnp.where(lane < levels, high, jnp.where(lane < 2 * levels, middle, low))
    return jnp.where(lane < 3 * levels, piece, 0.0).astype(jnp.bfloat16)


def attend(
    query_ref,
    fresh_key_ref,
    fresh_value_ref,
    count_ref,
    fill_ref,
    ranking_ref,
    keys,
    values,
    by_head,
    out,
    finished,
):
    f32 = jnp.float32
    rows = query_ref.shape[0]
    pages, page, _ = keys.shape
    tokens = pages * page
    heads = QUERY_HEADS // KEY_VALUE_HEADS
    group = heads * rows
    iota = lambda shape, axis: lax.broadcasted_iota(jnp.int32, shape, axis)
    diagonal = iota((pages, pages), 0) == iota((pages, pages), 1)
    page_of_slot = jnp.sum(
        jnp.where(diagonal, ranking_ref[...].astype(f32), 0.0), axis=1, keepdims=True
    )
    token = iota((pages, tokens), 1)
    page_of_token = lax.div(token, page).astype(f32)
    slot = jnp.sum(
        jnp.where(page_of_token == page_of_slot, iota((pages, tokens), 0).astype(f32), 0.0),
        axis=0,
        keepdims=True,
    )
    place = slot * page + lax.rem(token[:1], page).astype(f32)
    below = iota((rows, rows), 1) < iota((rows, rows), 0)
    same = iota((rows, rows), 1) == iota((rows, rows), 0)
    counts = count_ref[...].astype(f32)
    lengths = (counts - 1.0) * page + fill_ref[...].astype(f32)
    first = page * jnp.sum(jnp.where(below, counts, 0.0), axis=1, keepdims=True)
    last = first + jnp.sum(jnp.where(same, lengths, 0.0), axis=1, keepdims=True)
    visible = (place >= first) & (place < last)
    bias = jnp.where(visible, 0.0, -jnp.inf)
    scale = 1.0 / math.sqrt(HEAD_SIZE)
    for g in range(KEY_VALUE_HEADS):
        features = slice(g * HEAD_SIZE, (g + 1) * HEAD_SIZE)
        for h in range(heads):
            at = (g * heads + h) * HEAD_SIZE
            by_head[h] = query_ref[:, at : at + HEAD_SIZE]
        query = by_head[...]
        fresh_key = fresh_key_ref[:, features].astype(f32)
        fresh_value = fresh_value_ref[:, features].astype(f32)
        own = scale * jnp.sum(query.astype(f32) * fresh_key[None], axis=2, keepdims=True)
        scores = lax.dot_general(
            query.reshape(group, HEAD_SIZE),
            keys[:, :, features].reshape(tokens, HEAD_SIZE),
            (((1,), (1,)), ((), ())),
            preferred_element_type=f32,
        )
        scores = scores.reshape(heads, rows, tokens) * scale + bias[None]
        highest = jnp.maximum(jnp.max(scores, axis=2, keepdims=True), own)
        raised = jnp.exp(scores - highest)
        own_raised = jnp.exp(own - highest)
        inverse = 1.0 / (jnp.sum(raised, axis=2, keepdims=True) + own_raised)
        mixed = jnp.dot(
            raised.astype(jnp.bfloat16).reshape(group, tokens),
            values[:, :, features].reshape(tokens, HEAD_SIZE),
            preferred_element_type=f32,
        )
        mixed = mixed.reshape(heads, rows, HEAD_SIZE) + own_raised * fresh_value[None]
        mixed = (mixed * inverse).astype(jnp.bfloat16)
        for h in range(heads):
            at = (g * heads + h) * HEAD_SIZE
            out[:, at : at + HEAD_SIZE] = mixed[h]
        finished(g)


def layer_kernel(
    n,
    chunks,
    query_ref,
    fresh_key_ref,
    fresh_value_ref,
    count_ref,
    fill_ref,
    ranking_ref,
    residual_ref,
    gain_ref,
    routes_ref,
    route_weight_ref,
    key_hbm,
    value_hbm,
    wo_hbm,
    wg_hbm,
    wu_hbm,
    wd_hbm,
    out_ref,
    keys,
    values,
    by_head,
    residual_out,
    gains,
    inverse,
    hidden_own,
    g1,
    g2,
    res,
    wo,
    wg,
    wu,
    wd,
    gate,
    upward,
    squares,
    act,
    part,
    from_core,
    from_y,
    from_z,
    w_sem,
    send1,
    recv1,
    send2,
    recv2,
    res_send,
    res_recv,
    core_send,
    core_recv,
    y_send,
    y_recv,
    z_send,
    z_recv,
):
    levels = n // 4
    rows = query_ref.shape[0]
    total = n * rows
    cols = D // n
    width = D // chunks
    me = lax.axis_index("expert")
    z = lax.div(me, 4)
    y = lax.rem(lax.div(me, 2), 2)
    c = lax.rem(me, 2)
    device = lambda zz, yy, cc: zz * 4 + yy * 2 + cc
    beside_y = device(z, 1 - y, c)
    beside_core = device(z, y, 1 - c)

    cache_copies = [
        pltpu.make_async_copy(key_hbm, keys, w_sem.at[4]),
        pltpu.make_async_copy(value_hbm, values, w_sem.at[5]),
    ]
    for copy in cache_copies:
        copy.start()
    weight_copies = [
        pltpu.make_async_copy(source, target, w_sem.at[i])
        for i, (source, target) in enumerate(
            ((wo_hbm, wo), (wg_hbm, wg), (wu_hbm, wu), (wd_hbm, wd))
        )
    ]
    for copy in weight_copies:
        copy.start()

    barrier = pltpu.get_barrier_semaphore()

    @pl.loop(1, n)
    def greet(k):
        pl.semaphore_signal(
            barrier, inc=1, device_id={"expert": lax.rem(me + k, n)}, device_id_type=MESH
        )

    def gather(buf, send, recv, slices, consume):
        pieces = range(len(slices))

        def copy(p, zz, yy, cc, way, target):
            return pltpu.make_async_remote_copy(
                src_ref=buf.at[(zz, yy, cc) + slices[p]],
                dst_ref=buf.at[(zz, yy, cc) + slices[p]],
                send_sem=send.at[p, way, zz, yy, cc],
                recv_sem=recv.at[p, zz, yy, cc],
                device_id={"expert": target},
                device_id_type=MESH,
            )

        def up(p, zz):
            return copy(p, zz, y, c, 0, device(jnp.minimum(z + 1, levels - 1), y, c))

        def down(p, zz):
            return copy(p, zz, y, c, 1, device(jnp.maximum(z - 1, 0), y, c))

        def across(p, zz):
            return copy(p, zz, y, c, 2, beside_y)

        def beside(p, zz, yy):
            return copy(p, zz, yy, c, 3, beside_core)

        def landed(p, zz, yy, cc):
            copy(p, zz, yy, cc, 3, beside_core).wait_recv()

        def line(p, zz):
            @pl.when((zz <= z) & (z < levels - 1))
            def _():
                up(p, zz).start()

            @pl.when((zz >= z) & (z > 0))
            def _():
                down(p, zz).start()

            across(p, zz).start()
            beside(p, zz, y).start()

        def along(p, zz):
            landed(p, zz, y, c)
            line(p, zz)

        def crossed(p, zz):
            landed(p, zz, 1 - y, c)
            beside(p, zz, 1 - y).start()

        def at_distance(distance, body):
            @pl.loop(0, 2)
            def _(sign):
                zz = z - distance + 2 * distance * sign

                @pl.when(
                    (distance >= 0)
                    & (zz >= 0)
                    & (zz < levels)
                    & ((distance > 0) | (sign == 0))
                )
                def _():
                    body(zz)

        def start(p):
            line(p, z)

        def relay():
            if consume is not None:
                consume(z, y, c)

            @pl.loop(1, levels + 2)
            def step(s):
                for p in pieces:
                    at_distance(s, functools.partial(along, p))
                    at_distance(s - 1, functools.partial(crossed, p))
                if consume is not None:
                    at_distance(s, lambda zz: consume(zz, y, c))
                    at_distance(s - 1, lambda zz: consume(zz, 1 - y, c))

                def arrived(zz, yy):
                    for p in pieces:
                        landed(p, zz, yy, 1 - c)
                    if consume is not None:
                        consume(zz, yy, 1 - c)

                at_distance(s - 1, lambda zz: arrived(zz, y))
                at_distance(s - 2, lambda zz: arrived(zz, 1 - y))

        def drain():
            @pl.loop(0, levels)
            def _(zz):
                for p in pieces:

                    @pl.when((zz <= z) & (z < levels - 1))
                    def _():
                        up(p, zz).wait_send()

                    @pl.when((zz >= z) & (z > 0))
                    def _():
                        down(p, zz).wait_send()

                    across(p, zz).wait_send()
                    beside(p, zz, y).wait_send()
                    beside(p, zz, 1 - y).wait_send()

        return start, relay, drain

    half = D // 2
    columns = [(slice(None), pl.ds(0, half)), (slice(None), pl.ds(half, half + LANES))]
    start1, relay1, drain1 = gather(g1, send1, recv1, columns, None)

    def finished(g):
        if g == 0:
            pl.semaphore_wait(barrier, n - 1)
        start1(g)

    for d in range(n):
        at = slice(d * cols, (d + 1) * cols)
        residual_out[d] = residual_ref[:, at]
        gains[d] = gain_ref[at].astype(jnp.float32).reshape(1, cols)
        inverse[d] = 1.0 / gains[d]
    res[me] = residual_out[me]
    g1[z, y, c, :, D:] = packed_routes(levels, rows, routes_ref, route_weight_ref)
    for copy in cache_copies:
        copy.wait()
    attend(
        query_ref,
        fresh_key_ref,
        fresh_value_ref,
        count_ref,
        fill_ref,
        ranking_ref,
        keys,
        values,
        by_head,
        g1.at[z, y, c],
        finished,
    )

    def residual_copy(k):
        return pltpu.make_async_remote_copy(
            src_ref=residual_out.at[lax.rem(me + k, n)],
            dst_ref=res.at[me],
            send_sem=res_send.at[k],
            recv_sem=res_recv.at[me],
            device_id={"expert": lax.rem(me + k, n)},
            device_id_type=MESH,
        )

    def residual_landed(k):
        source = lax.rem(me + k, n)
        pltpu.make_async_remote_copy(
            src_ref=residual_out.at[source],
            dst_ref=res.at[source],
            send_sem=res_send.at[k],
            recv_sem=res_recv.at[source],
            device_id={"expert": source},
            device_id_type=MESH,
        ).wait_recv()

    @pl.loop(1, n)
    def _(k):
        residual_copy(k).start()

    relay1()
    weight_copies[0].wait()

    @pl.loop(1, n)
    def _(k):
        residual_landed(k)

    projected = jnp.zeros((total, cols), jnp.float32)
    for k in range(0, D, 1024):
        projected += jnp.dot(
            g1[:, :, :, :, k : k + 1024].reshape(total, 1024),
            wo[k : k + 1024, :],
            preferred_element_type=jnp.float32,
        )
    hidden = res[...].reshape(total, cols).astype(jnp.float32) + projected.astype(
        jnp.bfloat16
    ).astype(jnp.float32)
    g2[z, y, c] = (hidden * gains[me]).astype(jnp.bfloat16)
    gate[...] = jnp.zeros_like(gate)
    upward[...] = jnp.zeros_like(upward)
    squares[...] = jnp.zeros_like(squares)

    def consume(zz, yy, cc):
        d = device(zz, yy, cc)
        block = g2[zz, yy, cc]
        at = pl.ds(pl.multiple_of(d * cols, cols), cols)
        gate[...] += jnp.dot(block, wg[at, :], preferred_element_type=jnp.float32)
        upward[...] += jnp.dot(block, wu[at, :], preferred_element_type=jnp.float32)
        plain = block.astype(jnp.float32) * inverse[d]
        squares[...] += jnp.sum(plain * plain, axis=1, keepdims=True)

    share = total // 2
    strips = [(pl.ds(p * share, share), slice(None)) for p in range(2)]
    start2, relay2, drain2 = gather(g2, send2, recv2, strips, consume)
    for p in range(2):
        start2(p)
    weight_copies[1].wait()
    weight_copies[2].wait()
    relay2()
    scale = lax.rsqrt(squares[...] * (1.0 / D) + 1e-06)
    gated = gate[...] * scale
    act[...] = (gated / (1.0 + jnp.exp(-gated)) * (upward[...] * scale)).astype(jnp.bfloat16)
    table = g1[:, :, :, :, D : D + LANES].reshape(total, LANES).astype(jnp.float32)
    lane = lax.broadcasted_iota(jnp.int32, (total, LANES), 1)
    table = jnp.where((lane < 3 * levels) & (lax.rem(lane, levels) == z), table, 0.0)
    weight = jnp.sum(table, axis=1, keepdims=True)
    weight_copies[3].wait()

    def core_copy(j):
        return pltpu.make_async_remote_copy(
            src_ref=part.at[j, 1 - c],
            dst_ref=from_core.at[j],
            send_sem=core_send.at[j],
            recv_sem=core_recv.at[j],
            device_id={"expert": beside_core},
            device_id_type=MESH,
        )

    def y_copy(j):
        return pltpu.make_async_remote_copy(
            src_ref=part.at[j, c, 1 - y],
            dst_ref=from_y.at[j],
            send_sem=y_send.at[j],
            recv_sem=y_recv.at[j],
            device_id={"expert": beside_y},
            device_id_type=MESH,
        )

    def z_copy(j, goal):
        return pltpu.make_async_remote_copy(
            src_ref=part.at[j, c, y, goal],
            dst_ref=from_z.at[j, z],
            send_sem=z_send.at[j, goal],
            recv_sem=z_recv.at[j, z],
            device_id={"expert": device(goal, y, c)},
            device_id_type=MESH,
        )

    def z_landed(j, source):
        pltpu.make_async_remote_copy(
            src_ref=part.at[j, c, y, source],
            dst_ref=from_z.at[j, source],
            send_sem=z_send.at[j, source],
            recv_sem=z_recv.at[j, source],
            device_id={"expert": device(source, y, c)},
            device_id_type=MESH,
        ).wait_recv()

    def multiply(j):
        value = jnp.dot(
            act[...],
            wd[:, pl.ds(pl.multiple_of(j * width, width), width)],
            preferred_element_type=jnp.float32,
        )
        value = (value * weight).astype(jnp.bfloat16).reshape(levels, 2, 2, rows, width)
        for yy in range(2):
            for cc in range(2):
                part[j, cc, yy] = value[:, yy, cc]
        core_copy(j).start()

    def add_core(j):
        core_copy(j).wait_recv()
        for yy in range(2):
            part[j, c, yy] = (
                part[j, c, yy].astype(jnp.float32) + from_core[j, yy].astype(jnp.float32)
            ).astype(jnp.bfloat16)
        y_copy(j).start()

    def add_y(j):
        y_copy(j).wait_recv()
        part[j, c, y] = (
            part[j, c, y].astype(jnp.float32) + from_y[j].astype(jnp.float32)
        ).astype(jnp.bfloat16)

    def scatter(j):
        @pl.loop(1, levels)
        def _(k):
            z_copy(j, lax.rem(z + k, levels)).start()

    def finish(j):
        at = pl.ds(pl.multiple_of(j * width, width), width)
        hidden_own[:, at] += part[j, c, y, z].astype(jnp.float32)

        @pl.loop(1, levels)
        def _(k):
            source = lax.rem(z + k, levels)
            z_landed(j, source)
            hidden_own[:, at] += from_z[j, source].astype(jnp.float32)

        out_ref[:, at] = hidden_own[:, at].astype(jnp.bfloat16)

    @pl.loop(0, chunks + 1)
    def _(j):
        @pl.when(j < chunks)
        def _():
            multiply(j)

        @pl.when(j > 0)
        def _():
            add_core(j - 1)

    for d in range(n):
        mine = g2[d // 4, d // 2 % 2, d % 2, pl.ds(pl.multiple_of(me * rows, rows), rows), :]
        hidden_own[:, d * cols : (d + 1) * cols] = mine.astype(jnp.float32) * inverse[d]

    @pl.loop(0, chunks)
    def _(j):
        add_y(j)
        scatter(j)

    @pl.loop(0, chunks)
    def _(j):
        finish(j)

    drain1()
    drain2()

    @pl.loop(1, n)
    def _(k):
        residual_copy(k).wait_send()

    @pl.loop(0, chunks)
    def _(j):
        core_copy(j).wait_send()
        y_copy(j).wait_send()

        @pl.loop(0, levels)
        def _(goal):
            @pl.when(goal != z)
            def _():
                z_copy(j, goal).wait_send()


def layer(n, *operands):
    queries, keys, wo, wg, wu, wd = operands[0], operands[10], *operands[12:]
    rows = queries.shape[0]
    total = n * rows
    cols = wo.shape[1]
    hidden_units = wg.shape[1]
    levels = n // 4
    chunks = max(4, levels)
    width = D // chunks
    bf16, f32 = jnp.bfloat16, jnp.float32
    vmem = pl.BlockSpec(memory_space=pltpu.VMEM)
    dma = pltpu.SemaphoreType.DMA
    return pl.pallas_call(
        functools.partial(layer_kernel, n, chunks),
        out_shape=jax.ShapeDtypeStruct((rows, D), bf16),
        in_specs=[vmem] * 10 + [pl.BlockSpec(memory_space=pl.ANY)] * 6,
        out_specs=vmem,
        scratch_shapes=[
            pltpu.VMEM(keys.shape, bf16),
            pltpu.VMEM(keys.shape, bf16),
            pltpu.VMEM((QUERY_HEADS // KEY_VALUE_HEADS, rows, HEAD_SIZE), bf16),
            pltpu.VMEM((n, rows, cols), bf16),
            pltpu.VMEM((n, 1, cols), f32),
            pltpu.VMEM((n, 1, cols), f32),
            pltpu.VMEM((rows, D), f32),
            pltpu.VMEM((levels, 2, 2, rows, D + LANES), bf16),
            pltpu.VMEM((levels, 2, 2, total, cols), bf16),
            pltpu.VMEM((n, rows, cols), bf16),
            pltpu.VMEM(wo.shape, bf16),
            pltpu.VMEM(wg.shape, bf16),
            pltpu.VMEM(wu.shape, bf16),
            pltpu.VMEM(wd.shape, bf16),
            pltpu.VMEM((total, hidden_units), f32),
            pltpu.VMEM((total, hidden_units), f32),
            pltpu.VMEM((total, 1), f32),
            pltpu.VMEM((total, hidden_units), bf16),
            pltpu.VMEM((chunks, 2, 2, levels, rows, width), bf16),
            pltpu.VMEM((chunks, 2, levels, rows, width), bf16),
            pltpu.VMEM((chunks, levels, rows, width), bf16),
            pltpu.VMEM((chunks, levels, rows, width), bf16),
            dma((6,)),
            dma((2, 4, levels, 2, 2)),
            dma((2, levels, 2, 2)),
            dma((2, 4, levels, 2, 2)),
            dma((2, levels, 2, 2)),
            dma((n,)),
            dma((n,)),
            dma((chunks,)),
            dma((chunks,)),
            dma((chunks,)),
            dma((chunks,)),
            dma((chunks, levels)),
            dma((chunks, levels)),
        ],
        compiler_params=pltpu.CompilerParams(
            collective_id=0, has_side_effects=True, vmem_limit_bytes=62 * 1024 * 1024
        ),
        cost_estimate=pl.CostEstimate(
            flops=2 * total * D * (cols + 3 * hidden_units),
            bytes_accessed=2 * D * (cols + 3 * hidden_units),
            transcendentals=total * hidden_units,
        ),
    )(*operands)


def per_device(
    queries,
    fresh_key_rows,
    fresh_value_rows,
    key_cache_pages,
    value_cache_pages,
    sequence_page_table,
    last_page_fill,
    local_page_ranking,
    residual,
    out_weight,
    norm_gain,
    routes,
    route_weight,
    w_gate,
    w_up,
    w_down,
):
    return layer(
        lax.axis_size("expert"),
        queries,
        fresh_key_rows,
        fresh_value_rows,
        sequence_page_table,
        last_page_fill.reshape(1, -1),
        local_page_ranking,
        residual,
        norm_gain,
        routes.T,
        route_weight.T,
        key_cache_pages,
        value_cache_pages,
        out_weight,
        w_gate[0],
        w_up[0],
        w_down[0],
    )


def solution(mesh):
    return jax.shard_map(
        per_device,
        mesh=mesh,
        in_specs=(
            P(("group", "expert"), None),
            P(("group", "expert"), None),
            P(("group", "expert"), None),
            P(("group", "expert"), None, None),
            P(("group", "expert"), None, None),
            P(("group", "expert"), None),
            P(("group", "expert")),
            P(("group", "expert"), None),
            P(("group", "expert"), None),
            P(None, "expert"),
            P(),
            P(("group", "expert"), None),
            P(("group", "expert"), None),
            P("expert", None, None),
            P("expert", None, None),
            P("expert", None, None),
        ),
        out_specs=P(("group", "expert"), None),
        check_vma=False,
    )
```
